32 devices in a mesh: dp: 16 (over z, x, core), tensor: 2 (over y).
Axes of the slice: x: 2, y: 2, z: 4, core: 2. Of those that a mesh axis runs over, the one named last changes fastest.
Arguments:
- tokens: bfloat16 [16, 2048, 1024], P('dp', 'tensor'), may hold values from -6 to 6
- segment_ids: int32 [16, 2048], P('dp'), may hold values from 0 to 2047, as said below
- w_qkv: float32 [3, 1024, 1024], P(None, 'dp', 'tensor'), may hold values from -0.1875 to 0.1875
- w_out: float32 [1024, 1024], P('tensor', 'dp'), may hold values from -0.375 to 0.375
- w_in: float32 [1024, 4096], P('dp', 'tensor'), may hold values from -0.1875 to 0.1875
- w_back: float32 [4096, 1024], P('tensor', 'dp'), may hold values from -0.09375 to 0.09375
- norm_gains: float32 [2, 1024], P(None, 'dp'), may hold values from 0.1 to 1.9
- norm_biases: float32 [2, 1024], P(None, 'dp'), may hold values from -2 to 2
- cotangent: bfloat16 [16, 2048, 1024], P('dp', 'tensor'), may hold values from -6 to 6
Outputs:
- result: bfloat16 [16, 2048, 1024], P('dp', 'tensor')
- grad_tokens: bfloat16 [16, 2048, 1024], P('dp', 'tensor')
- grad_qkv: float32 [3, 1024, 1024], P(None, 'dp', 'tensor')
- grad_out: float32 [1024, 1024], P('tensor', 'dp')
- grad_in: float32 [1024, 4096], P('dp', 'tensor')
- grad_back: float32 [4096, 1024], P('tensor', 'dp')
- grad_gains: float32 [2, 1024], P(None, 'dp')
- grad_biases: float32 [2, 1024], P(None, 'dp')
The draws below stay inside these ranges and needn't reach their ends.
Inputs may be any that keep to these rules, and one draw needn't show every extreme that they name: `segment_ids`: A token's id is the position of its document's first token in its sequence, so ids never fall within a sequence; a token attends only to earlier tokens of its own id in its own sequence.
All inputs are finite; a program needn't handle non-finite values.
Results may differ from the reference program's by a relative error of at most 0.02.
Values may be sent and summed in bfloat16 or wider, within the bound.
No kernel may reach another device: no remote copies, remote signals or barrier semaphores. Data moves between devices by JAX's collectives and lax.ppermute only.
A program may use at most 256 MiB of HBM per device.

```python
import math
import jax
import jax.numpy as jnp
from jax import lax

D = 1024
HEADS = 8
HEAD = 128
FF = 4096
SEQ_LEN = 2048
SEQS = 16
ROW_BLOCK = 512


def draw_segment_ids(key, part):
    keys = jax.random.split(jax.random.fold_in(key, 17), 4)
    eighth = SEQ_LEN // 8
    first = jax.random.randint(keys[0], (SEQS, 1), 0, eighth)
    last = jax.random.randint(keys[1], (SEQS, 1), 7 * eighth + 1, SEQ_LEN + 1)
    rate = jax.random.randint(keys[2], (SEQS, 1), 6, 40)
    bits = jax.random.randint(keys[3], (SEQS, SEQ_LEN), 0, 1 << 20)
    pos = jnp.arange(SEQ_LEN, dtype=jnp.int32)[None, :]
    cut = bits % rate == 0
    outside = (pos < first) | (pos > last)
    flags = (pos == first) | (pos == last) | (pos == SEQ_LEN - 1) | cut & outside
    flags = flags & (pos > 0)
    starts = jnp.where(flags, pos, 0).astype(jnp.int32)
    starts = jnp.broadcast_to(starts, (SEQS, SEQ_LEN))
    return lax.cummax(starts, axis=1).astype(jnp.int32)


def shard_levels(stream_key, dims, cuts, least, top_value):
    loudness = 1.0
    for axis_at, blocks in cuts:
        heights = jax.random.uniform(jax.random.fold_in(jax.random.fold_in(stream_key, 6), axis_at), (blocks,), jnp.float32, least / len(cuts), top_value / len(cuts))
        loudness = loudness * jnp.repeat(jnp.exp(heights), dims[axis_at] // blocks).reshape((-1,) + (1,) * (len(dims) - 1 - axis_at))
    return loudness


def noise(own_key, dims, scale, most, cuts=(), kind=jnp.bfloat16):
    level = shard_levels(own_key, dims, cuts, -0.22, 0.18) if cuts else 1.0
    drawn = jax.random.normal(own_key, dims, jnp.float32) * scale * level
    return jnp.minimum(jnp.maximum(drawn, -most), most).astype(kind)


def setup_inputs(seed: int = 0) -> dict:
    key_of = jax.random.split(jax.random.key(seed), 10)
    return {
        "tokens": noise(key_of[0], (SEQS, SEQ_LEN, D), 1.0, 6.0, ((0, 16), (1, 2))),
        "segment_ids": draw_segment_ids(jax.random.fold_in(key_of[9], 71), 0),
        "w_qkv": noise(key_of[2], (3, D, D), D ** -0.5, 0.1875, ((1, 16), (2, 2)), jnp.float32),
        "w_out": noise(key_of[3], (D, D), (D // 4) ** -0.5, 0.375, ((0, 2), (1, 16)), jnp.float32),
        "w_in": noise(key_of[4], (D, FF), D ** -0.5, 0.1875, ((0, 16), (1, 2)), jnp.float32),
        "w_back": noise(key_of[5], (FF, D), FF ** -0.5, 0.09375, ((0, 2), (1, 16)), jnp.float32),
        "norm_gains": jnp.clip(1.0 + 0.18 * jax.random.normal(key_of[6], (2, D), jnp.float32), 0.1, 1.9),
        "norm_biases": noise(key_of[7], (2, D), 0.3, 2.0, ((1, 16),), jnp.float32),
        "cotangent": noise(key_of[8], (SEQS, SEQ_LEN, D), 1.0, 6.0, ((0, 16), (1, 2))),
    }


eps_norm = 1e-05
masked_score = -1e+30
highest = lax.Precision.HIGHEST

@jax.custom_vjp
def low(v):
    return lax.optimization_barrier(v.astype(jnp.bfloat16)).astype(jnp.float32)

@jax.custom_vjp
def low_back(v):
    return v

def low_keep(v):
    return (low(v), None)

def low_pass(kept, grad):
    return (grad,)

def back_keep(v):
    return (v, None)

def back_low(kept, grad):
    return (low(grad),)
low.defvjp(low_keep, low_pass)
low_back.defvjp(back_keep, back_low)

def layer_norm(values, gain, shift):
    center = values - lax.optimization_barrier(jnp.mean(values, axis=-1, keepdims=True))
    spread = lax.optimization_barrier(jnp.mean(center * center, axis=-1, keepdims=True))
    return center * lax.rsqrt(spread + eps_norm) * gain + shift

def attend(query, keys, values, seg):
    slopes = jnp.exp2(-(jnp.arange(HEADS, dtype=jnp.int32) + 1).astype(jnp.float32))
    cols = jnp.arange(SEQ_LEN, dtype=jnp.int32)
    scale = 1.0 / math.sqrt(HEAD)

    def block(start):
        rows = lax.dynamic_slice_in_dim(query, start, ROW_BLOCK, 0)
        seg_rows = lax.dynamic_slice_in_dim(seg, start, ROW_BLOCK, 0)
        row_ids = start + jnp.arange(ROW_BLOCK, dtype=jnp.int32)
        raw = jnp.einsum('qhd,khd->hqk', rows, keys, precision=highest) * scale
        dist = (row_ids[:, None] - cols[None, :]).astype(jnp.float32)
        raw = low_back(raw - slopes[:, None, None] * dist[None])
        allowed = (cols[None, :] <= row_ids[:, None]) & (seg_rows[:, None] == seg[None, :])
        probs = jax.nn.softmax(jnp.where(allowed[None], raw, masked_score), axis=-1)
        return jnp.einsum('hqk,khd->qhd', low(probs), values, precision=highest)
    starts = jnp.arange(SEQ_LEN // ROW_BLOCK, dtype=jnp.int32) * ROW_BLOCK
    mixed = lax.map(jax.checkpoint(block), starts)
    return mixed.reshape(SEQ_LEN, HEADS * HEAD)

def forward(x_seq, params, seg):
    w_qkv, w_out, w_in, w_back, gains, shifts = [low(p) for p in params]
    first_normalized = low(layer_norm(x_seq, gains[0], shifts[0]))
    proj = low_back(low(jnp.einsum('td,cde->cte', first_normalized, w_qkv, precision=highest)))
    heads = proj.reshape(3, SEQ_LEN, HEADS, HEAD)
    attended_values = low_back(low(attend(heads[0], heads[1], heads[2], seg)))
    branch = low_back(jnp.dot(attended_values, w_out, precision=highest, preferred_element_type=jnp.float32))
    resid = x_seq + branch
    second_normalized = low(layer_norm(resid, gains[1], shifts[1]))
    pre = low_back(jnp.dot(second_normalized, w_in, precision=highest, preferred_element_type=jnp.float32))
    hidden_activations = low(jax.nn.gelu(pre, approximate=True))
    return resid + jnp.dot(hidden_activations, w_back, precision=highest, preferred_element_type=jnp.float32)

def reference(tokens, segment_ids, w_qkv, w_out, w_in, w_back, norm_gains, norm_biases, cotangent):
    params = (w_qkv, w_out, w_in, w_back, norm_gains, norm_biases)
    zero = jax.tree.map(jnp.zeros_like, params)

    def one(total, item):
        x_seq, seg, cot = item
        out, pull = jax.vjp(lambda xv, pr: forward(xv, pr, seg), x_seq.astype(jnp.float32), params)
        grad_x, grad_params = pull(cot.astype(jnp.float32))
        total = jax.tree.map(jnp.add, total, grad_params)
        return (total, (out.astype(jnp.bfloat16), grad_x.astype(jnp.bfloat16)))
    total, (outs, grads_x) = lax.scan(one, zero, (tokens, segment_ids, cotangent))
    return (outs, grads_x, total[0], total[1], total[2], total[3], total[4], total[5])
```

```python
import math

import jax
import jax.numpy as jnp
from jax import lax
from jax.experimental import pallas as pl
from jax.experimental.pallas import tpu as pltpu
from jax.sharding import PartitionSpec as P

HEAD = 128
ROW_BLOCK = 512


eps_norm = 1e-05
masked_score = -1e30


def layer_norm(values, gain, shift):
    center = values - jnp.mean(values, axis=-1, keepdims=True)
    spread = jnp.mean(center * center, axis=-1, keepdims=True)
    return center * lax.rsqrt(spread + eps_norm) * gain + shift


def smooth_act(values):
    return jax.nn.gelu(values, approximate=True)


def block_scores(query_rows, keys, seg_rows, seg_all, row_ids, slopes):
    scale = 1.0 / math.sqrt(HEAD)
    raw = jnp.einsum("qhd,khd->hqk", query_rows, keys, preferred_element_type=jnp.float32) * scale
    cols = jnp.arange(keys.shape[0], dtype=jnp.int32)
    dist = (row_ids[:, None] - cols[None, :]).astype(jnp.float32)
    raw = raw - slopes[:, None, None] * dist[None]
    allowed = (cols[None, :] <= row_ids[:, None]) & (seg_rows[:, None] == seg_all[None, :])
    return jnp.where(allowed[None], raw, masked_score)


def attend_forward(qkv_seq, seg_seq, slopes):
    query, keys, values = (qkv_seq[0], qkv_seq[1], qkv_seq[2])
    length = keys.shape[0]

    def one_block(start):
        rows = lax.dynamic_slice_in_dim(query, start, ROW_BLOCK, 0)
        seg_rows = lax.dynamic_slice_in_dim(seg_seq, start, ROW_BLOCK, 0)
        row_ids = start + jnp.arange(ROW_BLOCK, dtype=jnp.int32)
        scores = block_scores(rows, keys, seg_rows, seg_seq, row_ids, slopes)
        top = jnp.max(scores, axis=-1, keepdims=True)
        expo = jnp.exp(scores - top)
        total = jnp.sum(expo, axis=-1, keepdims=True)
        probs = (expo / total).astype(jnp.bfloat16)
        mixed = jnp.einsum("hqk,khd->qhd", probs, values, preferred_element_type=jnp.float32)
        return (mixed, (top + jnp.log(total))[..., 0])

    starts = jnp.arange(length // ROW_BLOCK, dtype=jnp.int32) * ROW_BLOCK
    mixed, log_totals = lax.map(one_block, starts)
    return (mixed.reshape(length, -1), log_totals)


def attend_backward(qkv_seq, seg_seq, log_totals, grad_mixed, slopes):
    query, keys, values = (qkv_seq[0], qkv_seq[1], qkv_seq[2])
    length, heads_here, head_size = keys.shape
    scale = 1.0 / math.sqrt(HEAD)
    grad_rows_all = grad_mixed.reshape(length, heads_here, head_size)

    def one_block(carry, item):
        start, block_totals = item
        rows = lax.dynamic_slice_in_dim(query, start, ROW_BLOCK, 0)
        seg_rows = lax.dynamic_slice_in_dim(seg_seq, start, ROW_BLOCK, 0)
        grad_rows = lax.dynamic_slice_in_dim(grad_rows_all, start, ROW_BLOCK, 0)
        row_ids = start + jnp.arange(ROW_BLOCK, dtype=jnp.int32)
        scores = block_scores(rows, keys, seg_rows, seg_seq, row_ids, slopes)
        probs = jnp.exp(scores - block_totals[..., None])
        grad_probs = jnp.einsum(
            "qhd,khd->hqk", grad_rows, values, preferred_element_type=jnp.float32
        )
        inner = jnp.sum(probs * grad_probs, axis=-1, keepdims=True)
        grad_scores = (probs * (grad_probs - inner)).astype(jnp.bfloat16)
        grad_query = (
            jnp.einsum("hqk,khd->qhd", grad_scores, keys, preferred_element_type=jnp.float32)
            * scale
        )
        grad_keys = (
            carry[0]
            + jnp.einsum("hqk,qhd->khd", grad_scores, rows, preferred_element_type=jnp.float32)
            * scale
        )
        grad_values = carry[1] + jnp.einsum(
            "hqk,qhd->khd",
            probs.astype(jnp.bfloat16),
            grad_rows,
            preferred_element_type=jnp.float32,
        )
        return ((grad_keys, grad_values), grad_query)

    empty = jnp.zeros((length, heads_here, head_size), jnp.float32)
    starts = jnp.arange(length // ROW_BLOCK, dtype=jnp.int32) * ROW_BLOCK
    (grad_keys, grad_values), grad_query = lax.scan(one_block, (empty, empty), (starts, log_totals))
    return jnp.stack([grad_query.reshape(length, heads_here, head_size), grad_keys, grad_values])


def shards(tokens, segment_ids, w_qkv, w_out, w_in, w_back, norm_gains, norm_biases, cotangent):
    low_copies = (
        w_qkv.astype(jnp.bfloat16),
        w_out.astype(jnp.bfloat16),
        w_in.astype(jnp.bfloat16),
        w_back.astype(jnp.bfloat16),
        norm_gains.astype(jnp.bfloat16),
        norm_biases.astype(jnp.bfloat16),
    )
    (
        complete_query_key_value,
        complete_out_weight,
        complete_in_weight,
        complete_back_weight,
        gains_low,
        shifts_low,
    ) = (
        lax.all_gather(low_copies[0], "dp", axis=1, tiled=True),
        lax.all_gather(low_copies[1], "dp", axis=1, tiled=True),
        lax.all_gather(low_copies[2], "dp", axis=0, tiled=True),
        lax.all_gather(low_copies[3], "dp", axis=1, tiled=True),
        lax.all_gather(low_copies[4], "dp", axis=1, tiled=True),
        lax.all_gather(low_copies[5], "dp", axis=1, tiled=True),
    )
    gains = gains_low.astype(jnp.float32)
    shifts = shifts_low.astype(jnp.float32)
    seqs, own_len, width = tokens.shape
    length = segment_ids.shape[1]
    local_width = complete_query_key_value.shape[2]
    heads_here = local_width // HEAD
    rank = lax.axis_index("tensor")
    first_row = rank * own_len
    slopes = jnp.exp2(
        -(rank * heads_here + jnp.arange(heads_here, dtype=jnp.int32) + 1).astype(jnp.float32)
    )
    tokens_f = tokens.astype(jnp.float32)
    tokens_all = lax.all_gather(tokens, "tensor", axis=1, tiled=True).astype(jnp.float32)
    first_normalized = layer_norm(tokens_all, gains[0], shifts[0]).astype(jnp.bfloat16)
    projected = jnp.einsum(
        "gqu,fuk->gfqk",
        first_normalized,
        complete_query_key_value,
        preferred_element_type=jnp.float32,
    ).astype(jnp.bfloat16)
    qkv_heads = projected.reshape(seqs, 3, length, heads_here, HEAD)

    def forward_seq(item):
        return attend_forward(item[0], item[1], slopes)

    mixed, log_totals = lax.map(forward_seq, (qkv_heads, segment_ids))
    attended_values = mixed.astype(jnp.bfloat16)
    attention_slice = jnp.einsum(
        "oin,nh->oih", attended_values, complete_out_weight, preferred_element_type=jnp.float32
    )
    attn_all = lax.psum(attention_slice.astype(jnp.bfloat16), "tensor").astype(jnp.float32)
    resid_all = tokens_all + attn_all
    second_normalized = layer_norm(resid_all, gains[1], shifts[1]).astype(jnp.bfloat16)
    resid = lax.dynamic_slice_in_dim(resid_all, first_row, own_len, 1)
    hidden_preactivation = jnp.einsum(
        "rhi,ip->rhp", second_normalized, complete_in_weight, preferred_element_type=jnp.float32
    )
    hidden_activations = smooth_act(hidden_preactivation).astype(jnp.bfloat16)
    feedforward_slice = jnp.einsum(
        "cow,wv->cov", hidden_activations, complete_back_weight, preferred_element_type=jnp.float32
    )
    ffn_own = lax.psum_scatter(
        feedforward_slice.astype(jnp.bfloat16), "tensor", scatter_dimension=1, tiled=True
    ).astype(jnp.float32)
    result = (resid + ffn_own).astype(jnp.bfloat16)
    cotangent_gathered = lax.all_gather(cotangent, "tensor", axis=1, tiled=True)
    back_weight_gradient_shard = jnp.einsum(
        "ine,inb->eb", hidden_activations, cotangent_gathered, preferred_element_type=jnp.float32
    )
    hidden_gradient = jnp.einsum(
        "jrx,gx->jrg", cotangent_gathered, complete_back_weight, preferred_element_type=jnp.float32
    )
    _, act_pull = jax.vjp(smooth_act, hidden_preactivation)
    preactivation_gradient = act_pull(hidden_gradient)[0].astype(jnp.bfloat16)
    in_weight_gradient_shard = jnp.einsum(
        "bkw,bkz->wz", second_normalized, preactivation_gradient, preferred_element_type=jnp.float32
    )
    second_norm_slice = jnp.einsum(
        "kyj,tj->kyt",
        preactivation_gradient,
        complete_in_weight,
        preferred_element_type=jnp.float32,
    )
    grad_norm2 = lax.psum_scatter(
        second_norm_slice.astype(jnp.bfloat16), "tensor", scatter_dimension=1, tiled=True
    ).astype(jnp.float32)
    _, second_pull = jax.vjp(layer_norm, resid, gains[1], shifts[1])
    grad_resid_norm, grad_gain2, grad_shift2 = second_pull(grad_norm2)
    grad_resid = cotangent.astype(jnp.float32) + grad_resid_norm
    attention_gradient_gathered = lax.all_gather(
        grad_resid.astype(jnp.bfloat16), "tensor", axis=1, tiled=True
    )
    grad_out_local = jnp.einsum(
        "xwq,xwr->qr",
        attended_values,
        attention_gradient_gathered,
        preferred_element_type=jnp.float32,
    )
    grad_attended = jnp.einsum(
        "wik,jk->wij",
        attention_gradient_gathered,
        complete_out_weight,
        preferred_element_type=jnp.float32,
    ).astype(jnp.bfloat16)

    def backward_seq(item):
        return attend_backward(item[0], item[1], item[2], item[3], slopes)

    grad_heads = lax.map(backward_seq, (qkv_heads, segment_ids, log_totals, grad_attended))
    projection_gradient = grad_heads.reshape(seqs, 3, length, local_width).astype(jnp.bfloat16)
    grad_qkv_local = jnp.einsum(
        "phb,pthw->tbw", first_normalized, projection_gradient, preferred_element_type=jnp.float32
    )
    norm1_part = jnp.einsum(
        "zjyw,juw->zyu",
        projection_gradient,
        complete_query_key_value,
        preferred_element_type=jnp.float32,
    )
    grad_norm1 = lax.psum_scatter(
        norm1_part.astype(jnp.bfloat16), "tensor", scatter_dimension=1, tiled=True
    ).astype(jnp.float32)
    _, first_pull = jax.vjp(layer_norm, tokens_f, gains[0], shifts[0])
    grad_tok_norm, grad_gain1, grad_shift1 = first_pull(grad_norm1)
    grad_tokens = (grad_resid + grad_tok_norm).astype(jnp.bfloat16)
    gain_terms = jnp.stack([grad_gain1, grad_gain2])
    shift_terms = jnp.stack([grad_shift1, grad_shift2])
    gain_sum, shift_sum = lax.psum((gain_terms, shift_terms), "tensor")
    summed = (
        lax.psum_scatter(
            grad_qkv_local.astype(jnp.bfloat16), "dp", scatter_dimension=1, tiled=True
        ).astype(jnp.float32),
        lax.psum_scatter(
            grad_out_local.astype(jnp.bfloat16), "dp", scatter_dimension=1, tiled=True
        ).astype(jnp.float32),
        lax.psum_scatter(
            in_weight_gradient_shard.astype(jnp.bfloat16), "dp", scatter_dimension=0, tiled=True
        ).astype(jnp.float32),
        lax.psum_scatter(
            back_weight_gradient_shard.astype(jnp.bfloat16), "dp", scatter_dimension=1, tiled=True
        ).astype(jnp.float32),
        lax.psum_scatter(
            gain_sum.astype(jnp.bfloat16), "dp", scatter_dimension=1, tiled=True
        ).astype(jnp.float32),
        lax.psum_scatter(
            shift_sum.astype(jnp.bfloat16), "dp", scatter_dimension=1, tiled=True
        ).astype(jnp.float32),
    )
    return (result, grad_tokens, summed[0], summed[1], summed[2], summed[3], summed[4], summed[5])


LOG2E = math.log2(math.e)
SCALE2 = LOG2E / math.sqrt(HEAD)
BLK = 512
BF = jnp.bfloat16
F32 = jnp.float32
NN = (((1,), (0,)), ((), ()))
NT = (((1,), (1,)), ((), ()))
TN = (((0,), (0,)), ((), ()))
RING = (0, 2, 4, 6, 7, 5, 3, 1)


def mm(a, b, dims):
    return lax.dot_general(a, b, dims, preferred_element_type=F32)


def params(mib, cost=None):
    return dict(compiler_params=pltpu.CompilerParams(vmem_limit_bytes=mib * 2**20))


def cost(flops, nbytes, trans=0):
    return pl.CostEstimate(flops=int(flops), bytes_accessed=int(nbytes), transcendentals=int(trans))


def normalize(v):
    c = v - jnp.mean(v, axis=-1, keepdims=True)
    r = lax.rsqrt(jnp.mean(c * c, axis=-1, keepdims=True) + eps_norm)
    return c * r, r


def norm_back(v, dout, gain):
    cn, r = normalize(v)
    t = dout * gain
    dv = r * (t - jnp.mean(t, axis=-1, keepdims=True) - cn * jnp.mean(t * cn, axis=-1, keepdims=True))
    return dv, jnp.sum(dout * cn, axis=0, keepdims=True), jnp.sum(dout, axis=0, keepdims=True)


def project_kernel(core, xa, xb, gb, w, a1_out, qkv_out):
    step = pl.program_id(0)
    half = pl.num_programs(0) // 2
    x = jnp.where(step < half, xa[...], xb[...]).astype(F32)
    a1 = (normalize(x)[0] * gb[0:1] + gb[2:3]).astype(BF)
    a1_out[...] = a1
    weight = w[:, 0].reshape(w.shape[0] * w.shape[2], w.shape[3])
    qkv_out[...] = mm(a1, weight, NN).astype(BF)


def project(core, x_own, x_oth, gb, g1):
    rows, width = x_own.shape
    tile = 512
    half = rows // tile
    nd, _, per, cols = g1.shape
    wide = 3 * 512
    spec = pltpu.PrefetchScalarGridSpec(
        num_scalar_prefetch=1,
        grid=(2 * half,),
        in_specs=[
            pl.BlockSpec((tile, width), lambda i, c: (jnp.minimum(i, half - 1), 0)),
            pl.BlockSpec((tile, width), lambda i, c: (jnp.maximum(i - half, 0), 0)),
            pl.BlockSpec((4, width), lambda i, c: (0, 0)),
            pl.BlockSpec((nd, 1, per, wide), lambda i, c: (0, c[0], 0, 0)),
        ],
        out_specs=[
            pl.BlockSpec((tile, width), lambda i, c: (i % half + half * ((i // half) ^ c[0]), 0)),
            pl.BlockSpec((tile, wide), lambda i, c: (i % half + half * ((i // half) ^ c[0]), 0)),
        ],
    )
    return pl.pallas_call(
        project_kernel,
        grid_spec=spec,
        out_shape=[
            jax.ShapeDtypeStruct((2 * rows, width), BF),
            jax.ShapeDtypeStruct((2 * rows, wide), BF),
        ],
        cost_estimate=cost(4 * rows * width * wide, 12 * 2**20),
        **params(48),
    )(core, x_own, x_oth, gb, g1)


def attend_kernel(slopes, q_ref, k_ref, v_ref, seg_ref, o_ref, l_ref, s_ref):
    m2 = slopes[pl.program_id(0)]
    blocks = q_ref.shape[0] // BLK
    lane = lax.broadcasted_iota(jnp.int32, (1, BLK), 1)
    row = lax.broadcasted_iota(jnp.int32, (BLK, 1), 0)
    for i in range(blocks):
        q = q_ref[i * BLK : (i + 1) * BLK, :]
        seg = seg_ref[i * BLK : (i + 1) * BLK, :]
        top = jnp.full((BLK, 128), masked_score, F32)
        for j in range(i + 1):
            cols = slice(j * BLK, (j + 1) * BLK)
            bias = m2 * (lane + (j - i) * BLK).astype(F32)
            s = mm(q, k_ref[cols, :], NT) * SCALE2 + bias
            allowed = (lane + j * BLK) >= seg
            if j == i:
                allowed = allowed & (lane <= row)
            s = jnp.where(allowed, s, masked_score)
            s_ref[:, cols] = s
            for c in range(0, BLK, 128):
                top = jnp.maximum(top, s[:, c : c + 128])
        top = jnp.max(top, axis=1, keepdims=True)
        total = jnp.zeros((BLK, 128), F32)
        mixed = jnp.zeros((BLK, HEAD), F32)
        for j in range(i + 1):
            cols = slice(j * BLK, (j + 1) * BLK)
            p = jnp.exp2(s_ref[:, cols] - top)
            for c in range(0, BLK, 128):
                total = total + p[:, c : c + 128]
            mixed = mixed + mm(p.astype(BF), v_ref[cols, :], NN)
        total = jnp.sum(total, axis=1, keepdims=True)
        o_ref[i * BLK : (i + 1) * BLK, :] = (mixed / total).astype(BF)
        logs = jnp.broadcast_to(top + jnp.log2(total), (BLK, 128))
        l_ref[0, :, i * BLK : (i + 1) * BLK] = logs.T[0:1, :]


def attend(slopes, qkv, seg_col):
    length = qkv.shape[0]
    heads = qkv.shape[1] // (3 * HEAD)
    spec = pltpu.PrefetchScalarGridSpec(
        num_scalar_prefetch=1,
        grid=(heads,),
        in_specs=[
            pl.BlockSpec((length, HEAD), lambda h, s: (0, h)),
            pl.BlockSpec((length, HEAD), lambda h, s: (0, heads + h)),
            pl.BlockSpec((length, HEAD), lambda h, s: (0, 2 * heads + h)),
            pl.BlockSpec((length, 1), lambda h, s: (0, 0)),
        ],
        out_specs=[
            pl.BlockSpec((length, HEAD), lambda h, s: (0, h)),
            pl.BlockSpec((1, 1, length), lambda h, s: (h, 0, 0)),
        ],
        scratch_shapes=[pltpu.VMEM((BLK, length), F32)],
    )
    return pl.pallas_call(
        attend_kernel,
        grid_spec=spec,
        out_shape=[
            jax.ShapeDtypeStruct((length, heads * HEAD), BF),
            jax.ShapeDtypeStruct((heads, 1, length), F32),
        ],
        cost_estimate=cost(heads * 4 * length * length * HEAD, 10 * 2**20, heads * length * length),
        **params(48),
    )(slopes, qkv, qkv, qkv, seg_col)


def attend_back_kernel(slopes, q_ref, k_ref, v_ref, do_ref, o_ref, l_ref, seg_ref, dq_ref, dk_ref, dv_ref, acc, inner):
    m2 = slopes[pl.program_id(0)]
    blocks = q_ref.shape[0] // BLK
    lane = lax.broadcasted_iota(jnp.int32, (1, BLK), 1)
    row = lax.broadcasted_iota(jnp.int32, (BLK, 1), 0)
    for i in range(blocks):
        rows = slice(i * BLK, (i + 1) * BLK)
        d = jnp.sum(do_ref[rows, :].astype(F32) * o_ref[rows, :].astype(F32), axis=1, keepdims=True)
        inner[:, rows] = jnp.broadcast_to(d, (BLK, 128)).T[0:8, :]
    for j in range(blocks):
        cols = slice(j * BLK, (j + 1) * BLK)
        kj, vj = k_ref[cols, :], v_ref[cols, :]
        dk = jnp.zeros((BLK, HEAD), F32)
        dv = jnp.zeros((BLK, HEAD), F32)
        for i in range(j, blocks):
            rows = slice(i * BLK, (i + 1) * BLK)
            qi, doi = q_ref[rows, :], do_ref[rows, :]
            bias = m2 * (row + (j - i) * BLK).astype(F32)
            s = mm(kj, qi, NT) * SCALE2 + bias - l_ref[0, :, rows]
            allowed = (row + j * BLK) >= seg_ref[:, rows]
            if j == i:
                allowed = allowed & (row <= lane)
            p = jnp.exp2(jnp.where(allowed, s, masked_score))
            ds = (p * (mm(vj, doi, NT) - inner[0:1, rows])).astype(BF)
            dv = dv + mm(p.astype(BF), doi, NN)
            dk = dk + mm(ds, qi, NN)
            dq = mm(ds, kj, TN)
            if j == 0:
                acc[rows, :] = dq
            else:
                acc[rows, :] += dq
        dk_ref[cols, :] = (dk * (1.0 / math.sqrt(HEAD))).astype(BF)
        dv_ref[cols, :] = dv.astype(BF)
    dq_ref[...] = (acc[...] * (1.0 / math.sqrt(HEAD))).astype(BF)


def attend_back(slopes, qkv, grad, mixed, logs, seg_row, first, count):
    length = qkv.shape[0]
    heads = qkv.shape[1] // (3 * HEAD)
    spec = pltpu.PrefetchScalarGridSpec(
        num_scalar_prefetch=1,
        grid=(count,),
        in_specs=[
            pl.BlockSpec((length, HEAD), lambda h, s: (0, first + h)),
            pl.BlockSpec((length, HEAD), lambda h, s: (0, heads + first + h)),
            pl.BlockSpec((length, HEAD), lambda h, s: (0, 2 * heads + first + h)),
            pl.BlockSpec((length, HEAD), lambda h, s: (0, first + h)),
            pl.BlockSpec((length, HEAD), lambda h, s: (0, first + h)),
            pl.BlockSpec((1, 1, length), lambda h, s: (first + h, 0, 0)),
            pl.BlockSpec((1, length), lambda h, s: (0, 0)),
        ],
        out_specs=[pl.BlockSpec((length, HEAD), lambda h, s: (0, h))] * 3,
        scratch_shapes=[pltpu.VMEM((length, HEAD), F32), pltpu.VMEM((8, length), F32)],
    )
    return pl.pallas_call(
        attend_back_kernel,
        grid_spec=spec,
        out_shape=[jax.ShapeDtypeStruct((length, count * HEAD), BF)] * 3,
        cost_estimate=cost(count * 10 * length * length * HEAD, 5 * count * 2**20, count * length * length),
        **params(48),
    )(lax.slice_in_dim(slopes, first, first + count), qkv, qkv, qkv, grad, mixed, logs, seg_row)


def branch_kernel(core, o_ref, w, x_ref, oth_out, own_out):
    step = pl.program_id(0)
    half = pl.num_programs(0) // 2
    weight = w[:, 0].reshape(w.shape[0] * w.shape[2], w.shape[3])
    part = mm(o_ref[...], weight, NT)

    @pl.when(step < half)
    def _():
        oth_out[...] = part.astype(BF)

    @pl.when(step >= half)
    def _():
        own_out[...] = x_ref[...].astype(F32) + part


def branch(core, mixed, g1, x_own):
    rows, width = x_own.shape
    tile = 512
    half = rows // tile
    nd, _, per, cols = g1.shape
    spec = pltpu.PrefetchScalarGridSpec(
        num_scalar_prefetch=1,
        grid=(2 * half,),
        in_specs=[
            pl.BlockSpec((tile, 512), lambda i, c: (i % half + half * (1 - (i // half) ^ c[0]), 0)),
            pl.BlockSpec((nd, 1, per, 512), lambda i, c: (0, c[0], 0, 3)),
            pl.BlockSpec((tile, width), lambda i, c: (jnp.maximum(i - half, 0), 0)),
        ],
        out_specs=[
            pl.BlockSpec((tile, width), lambda i, c: (jnp.minimum(i, half - 1), 0)),
            pl.BlockSpec((tile, width), lambda i, c: (jnp.maximum(i - half, 0), 0)),
        ],
    )
    return pl.pallas_call(
        branch_kernel,
        grid_spec=spec,
        out_shape=[
            jax.ShapeDtypeStruct((rows, width), BF),
            jax.ShapeDtypeStruct((rows, width), F32),
        ],
        cost_estimate=cost(4 * rows * width * 512, 12 * 2**20),
        **params(48),
    )(core, mixed, g1, x_own)


def residual_kernel(part, recv, gb, h_out, a2_out):
    h = part[...] + recv[...].astype(F32)
    h_out[...] = h
    a2_out[...] = (normalize(h)[0] * gb[1:2] + gb[3:4]).astype(BF)


def residual(part, recv, gb):
    rows, width = part.shape
    tile = 256
    spec = pl.BlockSpec((tile, width), lambda i: (i, 0))
    return pl.pallas_call(
        residual_kernel,
        grid=(rows // tile,),
        in_specs=[spec, spec, pl.BlockSpec((4, width), lambda i: (0, 0))],
        out_specs=[spec, spec],
        out_shape=[
            jax.ShapeDtypeStruct((rows, width), F32),
            jax.ShapeDtypeStruct((rows, width), BF),
        ],
        cost_estimate=cost(20 * rows * width, 12 * 2**20),
        **params(32),
    )(part, recv, gb)


def feed_kernel(core, aa, ab, ya, yb, w1_ref, w2_ref, f_out, d_out, g1_out, g2_out, acc1, acc2, g_s, du_s):
    step = pl.program_id(0)
    steps = pl.num_programs(0)
    half = steps // 2
    hidden = w1_ref.shape[3]
    width = aa.shape[1]
    a2 = jnp.where(step < half, aa[...], ab[...])
    dy = jnp.where(step < half, ya[...], yb[...])
    a2t, dyt = a2.T, dy.T
    chunk = 512

    @pl.when(step == 0)
    def _():
        acc1[...] = jnp.zeros_like(acc1)
        acc2[...] = jnp.zeros_like(acc2)

    c0, c1 = math.sqrt(2.0 / math.pi), 0.044715
    for c in range(0, hidden, chunk):
        cols = slice(c, c + chunk)
        w1 = w1_ref[:, 0, :, cols].reshape(width, chunk)
        w2 = w2_ref[:, 0, :, cols].reshape(width, chunk)
        u = mm(a2, w1, NN)
        sq = u * u
        th = jnp.tanh(u * (c0 + c0 * c1 * sq))
        hp = 0.5 + 0.5 * th
        g = (u * hp).astype(BF)
        slope = hp + (0.5 * u) * (1.0 - th * th) * (c0 + 3.0 * c0 * c1 * sq)
        du = (mm(dy, w2, NN) * slope).astype(BF)
        g_s[:, cols] = g
        du_s[:, cols] = du
        acc1[:, cols] += mm(a2t, du, NN)
        acc2[:, cols] += mm(dyt, g, NN)
    f_out[0] = mm(g_s[...], w2_ref[:, 0].reshape(width, hidden), NT).astype(BF)
    d_out[0] = mm(du_s[...], w1_ref[:, 0].reshape(width, hidden), NT).astype(BF)

    @pl.when(step == steps - 1)
    def _():
        g1_out[:, 0] = acc1[...].astype(BF).reshape(g1_out.shape[0], g1_out.shape[2], hidden)
        g2_out[:, 0] = acc2[...].astype(BF).reshape(g1_out.shape[0], g1_out.shape[2], hidden)


def feed(core, a_own, a_oth, y_own, y_oth, w1, w2):
    rows, width = a_own.shape
    tile = 512
    half = rows // tile
    nd, _, per, hidden = w1.shape
    chips = nd // 2
    own = pl.BlockSpec((tile, width), lambda i, c: (jnp.minimum(i, half - 1), 0))
    oth = pl.BlockSpec((tile, width), lambda i, c: (jnp.maximum(i - half, 0), 0))
    weight = pl.BlockSpec((nd, 1, per, hidden), lambda i, c: (0, c[0], 0, 0), pipeline_mode=pl.Buffered(1))
    out = pl.BlockSpec((1, tile, width), lambda i, c: (i // half, i % half, 0))
    gout = pl.BlockSpec((chips, 1, 2 * per, hidden), lambda i, c: (0, 0, 0, 0), pipeline_mode=pl.Buffered(1))
    spec = pltpu.PrefetchScalarGridSpec(
        num_scalar_prefetch=1,
        grid=(2 * half,),
        in_specs=[own, oth, own, oth, weight, weight],
        out_specs=[out, out, gout, gout],
        scratch_shapes=[
            pltpu.VMEM((width, hidden), F32),
            pltpu.VMEM((width, hidden), F32),
            pltpu.VMEM((tile, hidden), BF),
            pltpu.VMEM((tile, hidden), BF),
        ],
    )
    return pl.pallas_call(
        feed_kernel,
        grid_spec=spec,
        out_shape=[
            jax.ShapeDtypeStruct((2, rows, width), BF),
            jax.ShapeDtypeStruct((2, rows, width), BF),
            jax.ShapeDtypeStruct((chips, 1, 2 * per, hidden), BF),
            jax.ShapeDtypeStruct((chips, 1, 2 * per, hidden), BF),
        ],
        cost_estimate=cost(24 * rows * width * hidden, 40 * 2**20, 2 * rows * hidden),
        **params(60),
    )(core, a_own, a_oth, y_own, y_oth, w1, w2)


def norm_back_kernel(v_ref, part, recv, skip, gain, dv_out, low_out, sums):
    @pl.when(pl.program_id(0) == 0)
    def _():
        sums[...] = jnp.zeros_like(sums)

    dout = part[...].astype(F32) + recv[...].astype(F32)
    dv, dg, db = norm_back(v_ref[...].astype(F32), dout, gain[...])
    dv = skip[...].astype(F32) + dv
    if dv_out is not None:
        dv_out[...] = dv
    low_out[...] = dv.astype(BF)
    sums[0:1] += dg
    sums[1:2] += db


def through_norm(v, part, recv, skip, gain, keep):
    rows, width = v.shape
    tile = 256
    spec = pl.BlockSpec((tile, width), lambda i: (i, 0))
    kernel = norm_back_kernel if keep else (lambda *r: norm_back_kernel(*r[:5], None, *r[5:]))
    outs = [jax.ShapeDtypeStruct((rows, width), F32)] if keep else []
    return pl.pallas_call(
        kernel,
        grid=(rows // tile,),
        in_specs=[spec] * 4 + [pl.BlockSpec((1, width), lambda i: (0, 0))],
        out_specs=[spec] * (1 + keep) + [pl.BlockSpec((2, width), lambda i: (0, 0))],
        out_shape=outs + [jax.ShapeDtypeStruct((rows, width), BF), jax.ShapeDtypeStruct((2, width), F32)],
        cost_estimate=cost(30 * rows * width, 16 * 2**20),
        **params(32),
    )(v, part, recv, skip, gain)


def head_grad_kernel(core, da, db, o_ref, w, do_out, gw_out, acc):
    step = pl.program_id(0)
    steps = pl.num_programs(0)
    d = jnp.where(step < steps // 2, da[...], db[...])
    weight = w[:, 0].reshape(w.shape[0] * w.shape[2], w.shape[3])
    do_out[...] = mm(d, weight, NN).astype(BF)

    @pl.when(step == 0)
    def _():
        acc[...] = jnp.zeros_like(acc)

    acc[...] += mm(d, o_ref[...], TN)

    @pl.when(step == steps - 1)
    def _():
        gw_out[...] = acc[...].astype(BF)


def head_grad(core, d_own, d_oth, mixed, g1):
    rows, width = d_own.shape
    tile = 512
    half = rows // tile
    nd, _, per, cols = g1.shape
    spec = pltpu.PrefetchScalarGridSpec(
        num_scalar_prefetch=1,
        grid=(2 * half,),
        in_specs=[
            pl.BlockSpec((tile, width), lambda i, c: (jnp.minimum(i, half - 1), 0)),
            pl.BlockSpec((tile, width), lambda i, c: (jnp.maximum(i - half, 0), 0)),
            pl.BlockSpec((tile, 512), lambda i, c: (i % half + half * ((i // half) ^ c[0]), 0)),
            pl.BlockSpec((nd, 1, per, 512), lambda i, c: (0, c[0], 0, 3)),
        ],
        out_specs=[
            pl.BlockSpec((tile, 512), lambda i, c: (i % half + half * ((i // half) ^ c[0]), 0)),
            pl.BlockSpec((width, 512), lambda i, c: (0, 0)),
        ],
        scratch_shapes=[pltpu.VMEM((width, 512), F32)],
    )
    return pl.pallas_call(
        head_grad_kernel,
        grid_spec=spec,
        out_shape=[
            jax.ShapeDtypeStruct((2 * rows, 512), BF),
            jax.ShapeDtypeStruct((width, 512), BF),
        ],
        cost_estimate=cost(8 * rows * width * 512, 12 * 2**20),
        **params(48),
    )(core, d_own, d_oth, mixed, g1)


def project_back_kernel(core, a1, q0, q1, k0, k1, v0, v1, w, d_oth, d_own, gw_out, acc):
    step = pl.program_id(0)
    steps = pl.num_programs(0)
    grad = jnp.concatenate([q0[...], q1[...], k0[...], k1[...], v0[...], v1[...]], axis=1)
    weight = w[:, 0].reshape(w.shape[0] * w.shape[2], w.shape[3])
    part = mm(grad, weight, NT)

    @pl.when(step < steps // 2)
    def _():
        d_oth[...] = part.astype(BF)

    @pl.when(step >= steps // 2)
    def _():
        d_own[...] = part

    @pl.when(step == 0)
    def _():
        acc[...] = jnp.zeros_like(acc)

    acc[...] += mm(a1[...], grad, TN)

    @pl.when(step == steps - 1)
    def _():
        gw_out[...] = acc[...].astype(BF)


def project_back(core, a1, grads, g1):
    rows2, width = a1.shape
    rows = rows2 // 2
    tile = 512
    half = rows // tile
    nd, _, per, cols = g1.shape
    wide = 3 * 512

    def place(i, c):
        return (i % half + half * (1 - (i // half) ^ c[0]), 0)

    spec = pltpu.PrefetchScalarGridSpec(
        num_scalar_prefetch=1,
        grid=(2 * half,),
        in_specs=[pl.BlockSpec((tile, width), place)]
        + [pl.BlockSpec((tile, g.shape[1]), place) for g in grads]
        + [pl.BlockSpec((nd, 1, per, wide), lambda i, c: (0, c[0], 0, 0))],
        out_specs=[
            pl.BlockSpec((tile, width), lambda i, c: (jnp.minimum(i, half - 1), 0)),
            pl.BlockSpec((tile, width), lambda i, c: (jnp.maximum(i - half, 0), 0)),
            pl.BlockSpec((width, wide), lambda i, c: (0, 0)),
        ],
        scratch_shapes=[pltpu.VMEM((width, wide), F32)],
    )
    return pl.pallas_call(
        project_back_kernel,
        grid_spec=spec,
        out_shape=[
            jax.ShapeDtypeStruct((rows, width), BF),
            jax.ShapeDtypeStruct((rows, width), F32),
            jax.ShapeDtypeStruct((width, wide), BF),
        ],
        cost_estimate=cost(8 * rows * width * wide, 20 * 2**20),
        **params(56),
    )(core, a1, *grads, g1)


def fast_shards(tokens, segment_ids, w_qkv, w_out, w_in, w_back, norm_gains, norm_biases, cotangent):
    both = ("dp", "tensor")
    dp_rank, y = lax.axis_index("dp"), lax.axis_index("tensor")
    n_dp = lax.axis_size("dp")
    core, chip = dp_rank % 2, dp_rank // 2
    chips = n_dp // 2
    at_home = core == y

    def ident(q, k, j):
        return (q * 2 + k) * 2 + j

    cells = [(q, k, j) for q in range(chips) for k in range(2) for j in range(2)]
    to_core = [(ident(q, k, j), ident(q, 1 - k, j)) for q, k, j in cells]
    to_y = [(ident(q, k, j), ident(q, k, 1 - j)) for q, k, j in cells]
    diagonal = [(ident(q, k, j), ident(q, j, k)) for q, k, j in cells]
    place_of = {q: p for p, q in enumerate(RING)}
    turn = {d: [(ident(q, k, j), ident(RING[(place_of[q] + d) % chips], k, j)) for q, k, j in cells] for d in (1, -1)}

    def send(v, pairs):
        return lax.ppermute(v, both, pairs)

    _, own_len, width = tokens.shape
    core_arg = core.astype(jnp.int32)[None]

    pad = jnp.zeros((norm_gains.shape[1], 124), BF)
    shard1 = jnp.concatenate(
        [w_qkv[0], w_qkv[1], w_qkv[2], w_out.T, norm_gains.T, norm_biases.T], axis=1
    ).astype(BF)
    shard1 = jnp.concatenate([shard1, pad], axis=1)
    shard2 = w_in.astype(BF)
    shard3 = w_back.T.astype(BF)
    g1 = lax.all_gather(shard1, both)
    shard2, shard3, g1 = lax.optimization_barrier((shard2, shard3, g1))
    w1 = lax.all_gather(shard2, both)
    w2 = lax.all_gather(shard3, both)
    g1, w1, w2 = [w.reshape(n_dp, 2, *w.shape[1:]) for w in (g1, w1, w2)]
    low = g1[:, 0, :, 2048:2052].reshape(width, 4).astype(F32).T
    gb = low

    seg = segment_ids
    seg = jnp.where(at_home, seg, send(seg, to_core))
    seg_col = seg.reshape(-1, 1)
    heads = w_qkv.shape[2] // HEAD
    slopes = jnp.exp2(-(core * heads + jnp.arange(heads, dtype=jnp.int32) + 1).astype(F32)) * LOG2E
    x_own = send(tokens[0], diagonal)
    x_oth = send(x_own, to_core)
    y_own = send(cotangent[0], diagonal)
    y_oth = send(y_own, to_core)

    a1, qkv = project(core_arg, x_own, x_oth, gb, g1)
    mixed, logs = attend(slopes, qkv, seg_col)
    part_oth, part_own = branch(core_arg, mixed, g1, x_own)
    h1, a2_own = residual(part_own, send(part_oth, to_core), gb)
    a2_oth = send(a2_own, to_core)
    f_part, d_part, gw1, gw2 = feed(core_arg, a2_own, a2_oth, y_own, y_oth, w1, w2)
    d_recv = send(d_part[1], to_core)
    f_recv = send(f_part[1], to_core)
    dh1, da_own, sums2 = through_norm(h1, d_part[0], d_recv, y_own, gb[1:2], True)
    da_oth = send(da_own, to_core)
    result = (h1 + f_part[0].astype(F32) + f_recv.astype(F32)).astype(BF)
    result = send(result, diagonal)
    do, gwo = head_grad(core_arg, da_own, da_oth, mixed, g1)
    parts = [attend_back(slopes, qkv, do, mixed, logs, seg, f, 2) for f in range(0, heads, 2)]
    grads = [p[i] for i in range(3) for p in parts]
    d1_oth, d1_own, gwq = project_back(core_arg, a1, grads, g1)
    grad_tokens, sums1 = through_norm(x_own, d1_own, send(d1_oth, to_core), dh1, gb[0:1], False)
    grad_tokens = send(grad_tokens, diagonal)

    spot = jnp.take(jnp.array([place_of[q] for q in range(chips)], jnp.int32), chip)
    order = jnp.array(RING, jnp.int32)

    def reduce_ring(blocks):
        def block(d):
            return lax.dynamic_index_in_dim(blocks, jnp.take(order, (spot + d) % chips), 0, keepdims=False)

        far = chips // 2
        rows = blocks.shape[1] // 2
        totals = []
        for way in (1, -1):
            piece = block(way * far)
            piece = piece[:rows] if way == 1 else piece[rows:]
            got = send(piece, turn[way])
            for d in range(far - 1, 0, -1):
                mine = block(way * d)
                if d == far - 1:
                    cut = slice(0, rows) if way == 1 else slice(rows, 2 * rows)
                    added = mine[cut].astype(F32) + got.astype(F32)
                    other = mine[rows:] if way == 1 else mine[:rows]
                    both_parts = [added.astype(BF), other] if way == 1 else [other, added.astype(BF)]
                    piece = jnp.concatenate(both_parts, axis=0)
                else:
                    piece = (mine.astype(F32) + got.astype(F32)).astype(BF)
                got = send(piece, turn[way])
            totals.append(got)
        return block(0).astype(F32) + totals[0].astype(F32) + totals[1].astype(F32)

    def to_owner(total):
        per = total.shape[0] // 2
        mine = lax.dynamic_slice_in_dim(total, core * per, per, 0)
        theirs = lax.dynamic_slice_in_dim(total, (1 - core) * per, per, 0).astype(BF)
        recv = send(theirs, to_core).astype(F32)
        keep = jnp.where(at_home, mine, recv)
        leave = jnp.where(at_home, recv, mine).astype(BF)
        return keep + send(leave, to_y).astype(F32)

    feed_blocks = jnp.concatenate([gw1, gw2], axis=1) if False else None
    r1 = to_owner(reduce_ring(gw1[:, 0]))
    r2 = to_owner(reduce_ring(gw2[:, 0]))
    r3 = to_owner(reduce_ring(jnp.concatenate([gwq, gwo], axis=1).reshape(chips, width // chips, -1)))
    grad_in = r1
    grad_back = r2.T
    per = r3.shape[0]
    grad_qkv = r3[:, : 3 * 512].reshape(per, 3, 512).transpose(1, 0, 2)
    grad_out = r3[:, 3 * 512 :].T
    sums = jnp.concatenate([sums1[0:1], sums2[0:1], sums1[1:2], sums2[1:2]], axis=0)
    sums = lax.psum(sums, both)
    sums = lax.dynamic_slice_in_dim(sums, dp_rank * norm_gains.shape[1], norm_gains.shape[1], 1)
    return (result[None], grad_tokens[None], grad_qkv, grad_out, grad_in, grad_back, sums[0:2], sums[2:4])


def solution(mesh):
    one_chip_plan = mesh.shape["dp"] == 16 and mesh.shape["tensor"] == 2
    return jax.shard_map(
        fast_shards if one_chip_plan else shards,
        mesh=mesh,
        in_specs=(
            P("dp", "tensor", None),
            P("dp", None),
            P(None, "dp", "tensor"),
            P("tensor", "dp"),
            P("dp", "tensor"),
            P("tensor", "dp"),
            P(None, "dp"),
            P(None, "dp"),
            P("dp", "tensor", None),
        ),
        out_specs=(
            P("dp", "tensor", None),
            P("dp", "tensor", None),
            P(None, "dp", "tensor"),
            P("tensor", "dp"),
            P("dp", "tensor"),
            P("tensor", "dp"),
            P(None, "dp"),
            P(None, "dp"),
        ),
        check_vma=False,
    )
```

```python
import math

import jax
import jax.numpy as jnp
from jax import lax
from jax.experimental import pallas as pl
from jax.experimental.pallas import tpu as pltpu
from jax.sharding import Mesh
from jax.sharding import PartitionSpec as P

HEAD = 128
ROW_BLOCK = 512


eps_norm = 1e-05
masked_score = -1e30


def layer_norm(values, gain, shift):
    center = values - jnp.mean(values, axis=-1, keepdims=True)
    spread = jnp.mean(center * center, axis=-1, keepdims=True)
    return center * lax.rsqrt(spread + eps_norm) * gain + shift


def smooth_act(values):
    return jax.nn.gelu(values, approximate=True)


def block_scores(query_rows, keys, seg_rows, seg_all, row_ids, slopes):
    scale = 1.0 / math.sqrt(HEAD)
    raw = jnp.einsum("qhd,khd->hqk", query_rows, keys, preferred_element_type=jnp.float32) * scale
    cols = jnp.arange(keys.shape[0], dtype=jnp.int32)
    dist = (row_ids[:, None] - cols[None, :]).astype(jnp.float32)
    raw = raw - slopes[:, None, None] * dist[None]
    allowed = (cols[None, :] <= row_ids[:, None]) & (seg_rows[:, None] == seg_all[None, :])
    return jnp.where(allowed[None], raw, masked_score)


def attend_forward(qkv_seq, seg_seq, slopes):
    query, keys, values = (qkv_seq[0], qkv_seq[1], qkv_seq[2])
    length = keys.shape[0]

    def one_block(start):
        rows = lax.dynamic_slice_in_dim(query, start, ROW_BLOCK, 0)
        seg_rows = lax.dynamic_slice_in_dim(seg_seq, start, ROW_BLOCK, 0)
        row_ids = start + jnp.arange(ROW_BLOCK, dtype=jnp.int32)
        scores = block_scores(rows, keys, seg_rows, seg_seq, row_ids, slopes)
        top = jnp.max(scores, axis=-1, keepdims=True)
        expo = jnp.exp(scores - top)
        total = jnp.sum(expo, axis=-1, keepdims=True)
        probs = (expo / total).astype(jnp.bfloat16)
        mixed = jnp.einsum("hqk,khd->qhd", probs, values, preferred_element_type=jnp.float32)
        return (mixed, (top + jnp.log(total))[..., 0])

    starts = jnp.arange(length // ROW_BLOCK, dtype=jnp.int32) * ROW_BLOCK
    mixed, log_totals = lax.map(one_block, starts)
    return (mixed.reshape(length, -1), log_totals)


def attend_backward(qkv_seq, seg_seq, log_totals, grad_mixed, slopes):
    query, keys, values = (qkv_seq[0], qkv_seq[1], qkv_seq[2])
    length, heads_here, head_size = keys.shape
    scale = 1.0 / math.sqrt(HEAD)
    grad_rows_all = grad_mixed.reshape(length, heads_here, head_size)

    def one_block(carry, item):
        start, block_totals = item
        rows = lax.dynamic_slice_in_dim(query, start, ROW_BLOCK, 0)
        seg_rows = lax.dynamic_slice_in_dim(seg_seq, start, ROW_BLOCK, 0)
        grad_rows = lax.dynamic_slice_in_dim(grad_rows_all, start, ROW_BLOCK, 0)
        row_ids = start + jnp.arange(ROW_BLOCK, dtype=jnp.int32)
        scores = block_scores(rows, keys, seg_rows, seg_seq, row_ids, slopes)
        probs = jnp.exp(scores - block_totals[..., None])
        grad_probs = jnp.einsum(
            "qhd,khd->hqk", grad_rows, values, preferred_element_type=jnp.float32
        )
        inner = jnp.sum(probs * grad_probs, axis=-1, keepdims=True)
        grad_scores = (probs * (grad_probs - inner)).astype(jnp.bfloat16)
        grad_query = (
            jnp.einsum("hqk,khd->qhd", grad_scores, keys, preferred_element_type=jnp.float32)
            * scale
        )
        grad_keys = (
            carry[0]
            + jnp.einsum("hqk,qhd->khd", grad_scores, rows, preferred_element_type=jnp.float32)
            * scale
        )
        grad_values = carry[1] + jnp.einsum(
            "hqk,qhd->khd",
            probs.astype(jnp.bfloat16),
            grad_rows,
            preferred_element_type=jnp.float32,
        )
        return ((grad_keys, grad_values), grad_query)

    empty = jnp.zeros((length, heads_here, head_size), jnp.float32)
    starts = jnp.arange(length // ROW_BLOCK, dtype=jnp.int32) * ROW_BLOCK
    (grad_keys, grad_values), grad_query = lax.scan(one_block, (empty, empty), (starts, log_totals))
    return jnp.stack([grad_query.reshape(length, heads_here, head_size), grad_keys, grad_values])


def shards(tokens, segment_ids, w_qkv, w_out, w_in, w_back, norm_gains, norm_biases, cotangent):
    low_copies = (
        w_qkv.astype(jnp.bfloat16),
        w_out.astype(jnp.bfloat16),
        w_in.astype(jnp.bfloat16),
        w_back.astype(jnp.bfloat16),
        norm_gains.astype(jnp.bfloat16),
        norm_biases.astype(jnp.bfloat16),
    )
    (
        complete_query_key_value,
        complete_out_weight,
        complete_in_weight,
        complete_back_weight,
        gains_low,
        shifts_low,
    ) = (
        lax.all_gather(low_copies[0], "dp", axis=1, tiled=True),
        lax.all_gather(low_copies[1], "dp", axis=1, tiled=True),
        lax.all_gather(low_copies[2], "dp", axis=0, tiled=True),
        lax.all_gather(low_copies[3], "dp", axis=1, tiled=True),
        lax.all_gather(low_copies[4], "dp", axis=1, tiled=True),
        lax.all_gather(low_copies[5], "dp", axis=1, tiled=True),
    )
    gains = gains_low.astype(jnp.float32)
    shifts = shifts_low.astype(jnp.float32)
    seqs, own_len, width = tokens.shape
    length = segment_ids.shape[1]
    local_width = complete_query_key_value.shape[2]
    heads_here = local_width // HEAD
    rank = lax.axis_index("tensor")
    first_row = rank * own_len
    slopes = jnp.exp2(
        -(rank * heads_here + jnp.arange(heads_here, dtype=jnp.int32) + 1).astype(jnp.float32)
    )
    tokens_f = tokens.astype(jnp.float32)
    tokens_all = lax.all_gather(tokens, "tensor", axis=1, tiled=True).astype(jnp.float32)
    first_normalized = layer_norm(tokens_all, gains[0], shifts[0]).astype(jnp.bfloat16)
    projected = jnp.einsum(
        "gqu,fuk->gfqk",
        first_normalized,
        complete_query_key_value,
        preferred_element_type=jnp.float32,
    ).astype(jnp.bfloat16)
    qkv_heads = projected.reshape(seqs, 3, length, heads_here, HEAD)

    def forward_seq(item):
        return attend_forward(item[0], item[1], slopes)

    mixed, log_totals = lax.map(forward_seq, (qkv_heads, segment_ids))
    attended_values = mixed.astype(jnp.bfloat16)
    attention_slice = jnp.einsum(
        "oin,nh->oih", attended_values, complete_out_weight, preferred_element_type=jnp.float32
    )
    attn_all = lax.psum(attention_slice.astype(jnp.bfloat16), "tensor").astype(jnp.float32)
    resid_all = tokens_all + attn_all
    second_normalized = layer_norm(resid_all, gains[1], shifts[1]).astype(jnp.bfloat16)
    resid = lax.dynamic_slice_in_dim(resid_all, first_row, own_len, 1)
    hidden_preactivation = jnp.einsum(
        "rhi,ip->rhp", second_normalized, complete_in_weight, preferred_element_type=jnp.float32
    )
    hidden_activations = smooth_act(hidden_preactivation).astype(jnp.bfloat16)
    feedforward_slice = jnp.einsum(
        "cow,wv->cov", hidden_activations, complete_back_weight, preferred_element_type=jnp.float32
    )
    ffn_own = lax.psum_scatter(
        feedforward_slice.astype(jnp.bfloat16), "tensor", scatter_dimension=1, tiled=True
    ).astype(jnp.float32)
    result = (resid + ffn_own).astype(jnp.bfloat16)
    cotangent_gathered = lax.all_gather(cotangent, "tensor", axis=1, tiled=True)
    back_weight_gradient_shard = jnp.einsum(
        "ine,inb->eb", hidden_activations, cotangent_gathered, preferred_element_type=jnp.float32
    )
    hidden_gradient = jnp.einsum(
        "jrx,gx->jrg", cotangent_gathered, complete_back_weight, preferred_element_type=jnp.float32
    )
    _, act_pull = jax.vjp(smooth_act, hidden_preactivation)
    preactivation_gradient = act_pull(hidden_gradient)[0].astype(jnp.bfloat16)
    in_weight_gradient_shard = jnp.einsum(
        "bkw,bkz->wz", second_normalized, preactivation_gradient, preferred_element_type=jnp.float32
    )
    second_norm_slice = jnp.einsum(
        "kyj,tj->kyt",
        preactivation_gradient,
        complete_in_weight,
        preferred_element_type=jnp.float32,
    )
    grad_norm2 = lax.psum_scatter(
        second_norm_slice.astype(jnp.bfloat16), "tensor", scatter_dimension=1, tiled=True
    ).astype(jnp.float32)
    _, second_pull = jax.vjp(layer_norm, resid, gains[1], shifts[1])
    grad_resid_norm, grad_gain2, grad_shift2 = second_pull(grad_norm2)
    grad_resid = cotangent.astype(jnp.float32) + grad_resid_norm
    attention_gradient_gathered = lax.all_gather(
        grad_resid.astype(jnp.bfloat16), "tensor", axis=1, tiled=True
    )
    grad_out_local = jnp.einsum(
        "xwq,xwr->qr",
        attended_values,
        attention_gradient_gathered,
        preferred_element_type=jnp.float32,
    )
    grad_attended = jnp.einsum(
        "wik,jk->wij",
        attention_gradient_gathered,
        complete_out_weight,
        preferred_element_type=jnp.float32,
    ).astype(jnp.bfloat16)

    def backward_seq(item):
        return attend_backward(item[0], item[1], item[2], item[3], slopes)

    grad_heads = lax.map(backward_seq, (qkv_heads, segment_ids, log_totals, grad_attended))
    projection_gradient = grad_heads.reshape(seqs, 3, length, local_width).astype(jnp.bfloat16)
    grad_qkv_local = jnp.einsum(
        "phb,pthw->tbw", first_normalized, projection_gradient, preferred_element_type=jnp.float32
    )
    norm1_part = jnp.einsum(
        "zjyw,juw->zyu",
        projection_gradient,
        complete_query_key_value,
        preferred_element_type=jnp.float32,
    )
    grad_norm1 = lax.psum_scatter(
        norm1_part.astype(jnp.bfloat16), "tensor", scatter_dimension=1, tiled=True
    ).astype(jnp.float32)
    _, first_pull = jax.vjp(layer_norm, tokens_f, gains[0], shifts[0])
    grad_tok_norm, grad_gain1, grad_shift1 = first_pull(grad_norm1)
    grad_tokens = (grad_resid + grad_tok_norm).astype(jnp.bfloat16)
    gain_terms = jnp.stack([grad_gain1, grad_gain2])
    shift_terms = jnp.stack([grad_shift1, grad_shift2])
    gain_sum, shift_sum = lax.psum((gain_terms, shift_terms), "tensor")
    summed = (
        lax.psum_scatter(
            grad_qkv_local.astype(jnp.bfloat16), "dp", scatter_dimension=1, tiled=True
        ).astype(jnp.float32),
        lax.psum_scatter(
            grad_out_local.astype(jnp.bfloat16), "dp", scatter_dimension=1, tiled=True
        ).astype(jnp.float32),
        lax.psum_scatter(
            in_weight_gradient_shard.astype(jnp.bfloat16), "dp", scatter_dimension=0, tiled=True
        ).astype(jnp.float32),
        lax.psum_scatter(
            back_weight_gradient_shard.astype(jnp.bfloat16), "dp", scatter_dimension=1, tiled=True
        ).astype(jnp.float32),
        lax.psum_scatter(
            gain_sum.astype(jnp.bfloat16), "dp", scatter_dimension=1, tiled=True
        ).astype(jnp.float32),
        lax.psum_scatter(
            shift_sum.astype(jnp.bfloat16), "dp", scatter_dimension=1, tiled=True
        ).astype(jnp.float32),
    )
    return (result, grad_tokens, summed[0], summed[1], summed[2], summed[3], summed[4], summed[5])


LOG2E = math.log2(math.e)
SCALE2 = LOG2E / math.sqrt(HEAD)
BLK = 512
BF = jnp.bfloat16
F32 = jnp.float32
NN = (((1,), (0,)), ((), ()))
NT = (((1,), (1,)), ((), ()))
TN = (((0,), (0,)), ((), ()))
RING = (0, 2, 4, 6, 7, 5, 3, 1)


def mm(a, b, dims):
    return lax.dot_general(a, b, dims, preferred_element_type=F32)


def params(mib, cost=None):
    return dict(compiler_params=pltpu.CompilerParams(vmem_limit_bytes=mib * 2**20))


def after(v, *deps):
    return lax.optimization_barrier((v,) + deps)[0]


def cost(flops, nbytes, trans=0):
    return pl.CostEstimate(flops=1024, bytes_accessed=1024, transcendentals=0)


def normalize(v):
    c = v - jnp.mean(v, axis=-1, keepdims=True)
    r = lax.rsqrt(jnp.mean(c * c, axis=-1, keepdims=True) + eps_norm)
    return c * r, r


def norm_back(v, dout, gain):
    cn, r = normalize(v)
    t = dout * gain
    dv = r * (t - jnp.mean(t, axis=-1, keepdims=True) - cn * jnp.mean(t * cn, axis=-1, keepdims=True))
    return dv, jnp.sum(dout * cn, axis=0, keepdims=True), jnp.sum(dout, axis=0, keepdims=True)


def project_kernel(core, xa, xb, gb, w, a1_out, qkv_out):
    step = pl.program_id(0)
    half = pl.num_programs(0) // 2
    x = jnp.where(step < half, xa[...], xb[...]).astype(F32)
    a1 = (normalize(x)[0] * gb[0:1] + gb[2:3]).astype(BF)
    a1_out[...] = a1
    weight = w[...].reshape(w.shape[0] * w.shape[1], w.shape[2])
    qkv_out[...] = mm(a1, weight, NN).astype(BF)


def project(core, x_own, x_oth, gb, g1):
    rows, width = x_own.shape
    tile = 512
    half = rows // tile
    chips, per, _ = g1.shape
    wide = 3 * 512
    spec = pltpu.PrefetchScalarGridSpec(
        num_scalar_prefetch=1,
        grid=(2 * half,),
        in_specs=[
            pl.BlockSpec((tile, width), lambda i, c: (jnp.minimum(i, half - 1), 0)),
            pl.BlockSpec((tile, width), lambda i, c: (jnp.maximum(i - half, 0), 0)),
            pl.BlockSpec((4, width), lambda i, c: (0, 0)),
            pl.BlockSpec((chips, per, wide), lambda i, c: (0, 0, 0)),
        ],
        out_specs=[
            pl.BlockSpec((tile, width), lambda i, c: (i % half + half * ((i // half) ^ c[0]), 0)),
            pl.BlockSpec((tile, wide), lambda i, c: (i % half + half * ((i // half) ^ c[0]), 0)),
        ],
    )
    return pl.pallas_call(
        project_kernel,
        grid_spec=spec,
        out_shape=[
            jax.ShapeDtypeStruct((2 * rows, width), BF),
            jax.ShapeDtypeStruct((2 * rows, wide), BF),
        ],
        cost_estimate=cost(4 * rows * width * wide, 12 * 2**20),
        **params(48),
    )(core, x_own, x_oth, gb, g1)


def attend_kernel(slopes, q_ref, k_ref, v_ref, seg_ref, o_ref, l_ref, s_ref):
    m2 = slopes[pl.program_id(0)]
    blocks = q_ref.shape[0] // BLK
    lane = lax.broadcasted_iota(jnp.int32, (1, BLK), 1)
    row = lax.broadcasted_iota(jnp.int32, (BLK, 1), 0)
    for i in range(blocks):
        q = q_ref[i * BLK : (i + 1) * BLK, :]
        seg = seg_ref[i * BLK : (i + 1) * BLK, :]
        top = jnp.full((BLK, 128), masked_score, F32)
        for j in range(i + 1):
            cols = slice(j * BLK, (j + 1) * BLK)
            bias = m2 * (lane + (j - i) * BLK).astype(F32)
            s = mm(q, k_ref[cols, :], NT) * SCALE2 + bias
            allowed = (lane + j * BLK) >= seg
            if j == i:
                allowed = allowed & (lane <= row)
            s = jnp.where(allowed, s, masked_score)
            s_ref[:, cols] = s
            for c in range(0, BLK, 128):
                top = jnp.maximum(top, s[:, c : c + 128])
        top = jnp.max(top, axis=1, keepdims=True)
        total = jnp.zeros((BLK, 128), F32)
        mixed = jnp.zeros((BLK, HEAD), F32)
        for j in range(i + 1):
            cols = slice(j * BLK, (j + 1) * BLK)
            p = jnp.exp2(s_ref[:, cols] - top)
            for c in range(0, BLK, 128):
                total = total + p[:, c : c + 128]
            mixed = mixed + mm(p.astype(BF), v_ref[cols, :], NN)
        total = jnp.sum(total, axis=1, keepdims=True)
        o_ref[i * BLK : (i + 1) * BLK, :] = (mixed / total).astype(BF)
        logs = jnp.broadcast_to(top + jnp.log2(total), (BLK, 128))
        l_ref[0, :, i * BLK : (i + 1) * BLK] = logs.T[0:1, :]


def attend(slopes, qkv, seg_col, first, count):
    length = qkv.shape[0]
    heads = qkv.shape[1] // (3 * HEAD)
    spec = pltpu.PrefetchScalarGridSpec(
        num_scalar_prefetch=1,
        grid=(count,),
        in_specs=[
            pl.BlockSpec((length, HEAD), lambda h, s: (0, first + h)),
            pl.BlockSpec((length, HEAD), lambda h, s: (0, heads + first + h)),
            pl.BlockSpec((length, HEAD), lambda h, s: (0, 2 * heads + first + h)),
            pl.BlockSpec((length, 1), lambda h, s: (0, 0)),
        ],
        out_specs=[
            pl.BlockSpec((length, HEAD), lambda h, s: (0, h)),
            pl.BlockSpec((1, 1, length), lambda h, s: (h, 0, 0)),
        ],
        scratch_shapes=[pltpu.VMEM((BLK, length), F32)],
    )
    return pl.pallas_call(
        attend_kernel,
        grid_spec=spec,
        out_shape=[
            jax.ShapeDtypeStruct((length, count * HEAD), BF),
            jax.ShapeDtypeStruct((count, 1, length), F32),
        ],
        cost_estimate=cost(count * 4 * length * length * HEAD, 3 * count * 2**20, count * length * length),
        **params(48),
    )(lax.slice_in_dim(slopes, first, first + count), qkv, qkv, qkv, seg_col)


def attend_back_kernel(slopes, q_ref, k_ref, v_ref, do_ref, o_ref, l_ref, seg_ref, dq_ref, dk_ref, dv_ref, acc, inner):
    m2 = slopes[pl.program_id(0)]
    blocks = q_ref.shape[0] // BLK
    lane = lax.broadcasted_iota(jnp.int32, (1, BLK), 1)
    row = lax.broadcasted_iota(jnp.int32, (BLK, 1), 0)
    for i in range(blocks):
        rows = slice(i * BLK, (i + 1) * BLK)
        d = jnp.sum(do_ref[rows, :].astype(F32) * o_ref[rows, :].astype(F32), axis=1, keepdims=True)
        inner[:, rows] = jnp.broadcast_to(d, (BLK, 128)).T[0:8, :]
    for j in range(blocks):
        cols = slice(j * BLK, (j + 1) * BLK)
        kj, vj = k_ref[cols, :], v_ref[cols, :]
        dk = jnp.zeros((BLK, HEAD), F32)
        dv = jnp.zeros((BLK, HEAD), F32)
        for i in range(j, blocks):
            rows = slice(i * BLK, (i + 1) * BLK)
            qi, doi = q_ref[rows, :], do_ref[rows, :]
            bias = m2 * (row + (j - i) * BLK).astype(F32)
            s = mm(kj, qi, NT) * SCALE2 + bias - l_ref[0, :, rows]
            allowed = (row + j * BLK) >= seg_ref[:, rows]
            if j == i:
                allowed = allowed & (row <= lane)
            p = jnp.exp2(jnp.where(allowed, s, masked_score))
            ds = (p * (mm(vj, doi, NT) - inner[0:1, rows])).astype(BF)
            dv = dv + mm(p.astype(BF), doi, NN)
            dk = dk + mm(ds, qi, NN)
            dq = mm(ds, kj, TN)
            if j == 0:
                acc[rows, :] = dq
            else:
                acc[rows, :] += dq
        dk_ref[cols, :] = (dk * (1.0 / math.sqrt(HEAD))).astype(BF)
        dv_ref[cols, :] = dv.astype(BF)
    dq_ref[...] = (acc[...] * (1.0 / math.sqrt(HEAD))).astype(BF)


def attend_back(slopes, qkv, grad, mixed, logs, seg_row):
    length = qkv.shape[0]
    heads = qkv.shape[1] // (3 * HEAD)

    def column(at):
        return pl.BlockSpec((length, HEAD), lambda h, s: (0, at + h))

    spec = pltpu.PrefetchScalarGridSpec(
        num_scalar_prefetch=1,
        grid=(heads,),
        in_specs=[
            column(0),
            column(heads),
            column(2 * heads),
            column(0),
            column(0),
            pl.BlockSpec((1, 1, length), lambda h, s: (h, 0, 0)),
            pl.BlockSpec((1, length), lambda h, s: (0, 0)),
        ],
        out_specs=[column(0)] * 3,
        scratch_shapes=[pltpu.VMEM((length, HEAD), F32), pltpu.VMEM((8, length), F32)],
    )
    return pl.pallas_call(
        attend_back_kernel,
        grid_spec=spec,
        out_shape=[jax.ShapeDtypeStruct((length, heads * HEAD), BF)] * 3,
        cost_estimate=cost(heads * 10 * length * length * HEAD, 5 * heads * 2**20, heads * length * length),
        **params(48),
    )(slopes, qkv, qkv, qkv, grad, mixed, logs, seg_row)


def branch_kernel(core, oa, ob, w, x_ref, oth_out, own_out):
    step = pl.program_id(0)
    half = pl.num_programs(0) // 2
    weight = w[...].reshape(w.shape[0] * w.shape[1], w.shape[2])
    part = mm(jnp.concatenate([oa[...], ob[...]], axis=1), weight, NT)

    @pl.when(step < half)
    def _():
        oth_out[...] = part.astype(BF)

    @pl.when(step >= half)
    def _():
        own_out[...] = x_ref[...].astype(F32) + part


def branch(core, mixed, g1, x_own):
    rows, width = x_own.shape
    tile = 512
    half = rows // tile
    chips, per, _ = g1.shape
    spec = pltpu.PrefetchScalarGridSpec(
        num_scalar_prefetch=1,
        grid=(2 * half,),
        in_specs=[
            pl.BlockSpec((tile, 256), lambda i, c: (i % half + half * (1 - (i // half) ^ c[0]), 0)),
            pl.BlockSpec((tile, 256), lambda i, c: (i % half + half * (1 - (i // half) ^ c[0]), 0)),
            pl.BlockSpec((chips, per, 512), lambda i, c: (0, 0, 3)),
            pl.BlockSpec((tile, width), lambda i, c: (jnp.maximum(i - half, 0), 0)),
        ],
        out_specs=[
            pl.BlockSpec((tile, width), lambda i, c: (jnp.minimum(i, half - 1), 0)),
            pl.BlockSpec((tile, width), lambda i, c: (jnp.maximum(i - half, 0), 0)),
        ],
    )
    return pl.pallas_call(
        branch_kernel,
        grid_spec=spec,
        out_shape=[
            jax.ShapeDtypeStruct((rows, width), BF),
            jax.ShapeDtypeStruct((rows, width), F32),
        ],
        cost_estimate=cost(4 * rows * width * 512, 12 * 2**20),
        **params(48),
    )(core, *mixed, g1, x_own)


def residual_kernel(part, recv, gb, h_out, a2_out):
    h = part[...] + recv[...].astype(F32)
    h_out[...] = h
    a2_out[...] = (normalize(h)[0] * gb[1:2] + gb[3:4]).astype(BF)


def residual(part, recv, gb):
    rows, width = part.shape
    tile = 256
    spec = pl.BlockSpec((tile, width), lambda i: (i, 0))
    return pl.pallas_call(
        residual_kernel,
        grid=(rows // tile,),
        in_specs=[spec, spec, pl.BlockSpec((4, width), lambda i: (0, 0))],
        out_specs=[spec, spec],
        out_shape=[
            jax.ShapeDtypeStruct((rows, width), F32),
            jax.ShapeDtypeStruct((rows, width), BF),
        ],
        cost_estimate=cost(20 * rows * width, 12 * 2**20),
        **params(32),
    )(part, recv, gb)


def up_kernel(core, aa, ab, ya, yb, w_ref, g_out, s_out, gw_out, acc):
    step = pl.program_id(0)
    steps = pl.num_programs(0)
    a2 = jnp.where(step < steps // 2, aa[...], ab[...])
    dyt = jnp.where(step < steps // 2, ya[...], yb[...]).T
    chips, per, hidden = w_ref.shape
    chunk = 512
    c0, c1 = math.sqrt(2.0 / math.pi), 0.044715

    @pl.when(step == 0)
    def _():
        acc[...] = jnp.zeros_like(acc)

    for c in range(0, hidden, chunk):
        cols = slice(c, c + chunk)
        u = mm(a2, w_ref[:, :, cols].reshape(chips * per, chunk), NN)
        sq = u * u
        th = jnp.tanh(u * (c0 + c0 * c1 * sq))
        hp = 0.5 + 0.5 * th
        g = (u * hp).astype(BF)
        g_out[:, cols] = g
        s_out[:, cols] = (hp + (0.5 * u) * (1.0 - th * th) * (c0 + 3.0 * c0 * c1 * sq)).astype(BF)
        acc[:, cols] += mm(dyt, g, NN)

    @pl.when(step == steps - 1)
    def _():
        gw_out[...] = acc[...].astype(BF).reshape(gw_out.shape)


def halves(tile, width, half):
    return [
        pl.BlockSpec((tile, width), lambda i, *c: (jnp.minimum(i, half - 1), 0)),
        pl.BlockSpec((tile, width), lambda i, *c: (jnp.maximum(i - half, 0), 0)),
    ]


def ringed(w):
    return pl.BlockSpec(w.shape, lambda i, *c: (0, 0, 0), pipeline_mode=pl.Buffered(1))


def gathered(w):
    return pl.BlockSpec((w.shape[0], 1) + w.shape[2:], lambda i, c: (0, c[0], 0, 0), pipeline_mode=pl.Buffered(1))


def up(core, a_own, a_oth, y_own, y_oth, w1):
    rows, width = a_own.shape
    chips, _, hidden = w1.shape
    tile = 512
    out = pl.BlockSpec((tile, hidden), lambda i, c: (i, 0))
    spec = pltpu.PrefetchScalarGridSpec(
        num_scalar_prefetch=1,
        grid=(2 * rows // tile,),
        in_specs=halves(tile, width, rows // tile) * 2 + [ringed(w1)],
        out_specs=[
            out,
            out,
            pl.BlockSpec((chips, width // chips, hidden), lambda i, c: (0, 0, 0), pipeline_mode=pl.Buffered(1)),
        ],
        scratch_shapes=[pltpu.VMEM((width, hidden), F32)],
    )
    return pl.pallas_call(
        up_kernel,
        grid_spec=spec,
        out_shape=[jax.ShapeDtypeStruct((2 * rows, hidden), BF)] * 2
        + [jax.ShapeDtypeStruct((chips, width // chips, hidden), BF)],
        cost_estimate=cost(8 * rows * width * hidden, 32 * 2**20, 2 * rows * hidden),
        **params(60),
    )(core, a_own, a_oth, y_own, y_oth, w1)


def down_kernel(core, aa, ab, ya, yb, g_ref, s_ref, w1_ref, w2_ref, f_own, f_oth, d_own, d_oth, gw_out, acc, du_s):
    step = pl.program_id(0)
    steps = pl.num_programs(0)
    half = steps // 2
    chips, per, hidden = w1_ref.shape
    width = chips * per
    a2t = jnp.where(step < half, aa[...], ab[...]).T
    dy = jnp.where(step < half, ya[...], yb[...])
    chunk = 512

    @pl.when(step == 0)
    def _():
        acc[...] = jnp.zeros_like(acc)

    for c in range(0, hidden, chunk):
        cols = slice(c, c + chunk)
        dg = mm(dy, w2_ref[:, 0, :, cols].reshape(width, chunk), NN)
        du = (dg * s_ref[:, cols].astype(F32)).astype(BF)
        du_s[:, cols] = du
        acc[:, cols] += mm(a2t, du, NN)
    f = mm(g_ref[...], w2_ref[:, 0].reshape(width, hidden), NT).astype(BF)
    d = mm(du_s[...], w1_ref[...].reshape(width, hidden), NT).astype(BF)

    @pl.when(step < half)
    def _():
        f_own[...] = f
        d_own[...] = d

    @pl.when(step >= half)
    def _():
        f_oth[...] = f
        d_oth[...] = d

    @pl.when(step == steps - 1)
    def _():
        gw_out[...] = acc[...].astype(BF).reshape(gw_out.shape)


def down(core, a_own, a_oth, y_own, y_oth, hidden_units, slope, w1, w2):
    rows, width = a_own.shape
    chips, per, hidden = w1.shape
    tile = 512
    units = pl.BlockSpec((tile, hidden), lambda i, c: (i, 0))
    spec = pltpu.PrefetchScalarGridSpec(
        num_scalar_prefetch=1,
        grid=(2 * rows // tile,),
        in_specs=halves(tile, width, rows // tile) * 2 + [units, units, ringed(w1), gathered(w2)],
        out_specs=halves(tile, width, rows // tile) * 2
        + [pl.BlockSpec((chips, per, hidden), lambda i, c: (0, 0, 0), pipeline_mode=pl.Buffered(1))],
        scratch_shapes=[pltpu.VMEM((width, hidden), F32), pltpu.VMEM((tile, hidden), BF)],
    )
    return pl.pallas_call(
        down_kernel,
        grid_spec=spec,
        out_shape=[jax.ShapeDtypeStruct((rows, width), BF)] * 4
        + [jax.ShapeDtypeStruct((chips, per, hidden), BF)],
        cost_estimate=cost(16 * rows * width * hidden, 40 * 2**20),
        **params(60),
    )(core, a_own, a_oth, y_own, y_oth, hidden_units, slope, w1, w2)


def assemble_kernel(order, *refs):
    *pieces, far_a, far_b, out, sems = refs
    half = far_a.shape[0]
    n = len(pieces)
    copies = [pltpu.make_async_copy(p, out.at[order[i]], sems.at[i]) for i, p in enumerate(pieces)]
    copies.append(pltpu.make_async_copy(far_a, out.at[order[n], pl.ds(0, half)], sems.at[n]))
    copies.append(pltpu.make_async_copy(far_b, out.at[order[n], pl.ds(half, half)], sems.at[n + 1]))
    for c in copies:
        c.start()
    for c in copies:
        c.wait()


def assemble(order, pieces, far_a, far_b):
    unit = pieces[0]
    any_ = pl.BlockSpec(memory_space=pl.ANY)
    spec = pltpu.PrefetchScalarGridSpec(
        num_scalar_prefetch=1,
        grid=(1,),
        in_specs=[pl.BlockSpec(p.shape, lambda i, o: (0, 0)) for p in (*pieces, far_a, far_b)],
        out_specs=any_,
        scratch_shapes=[pltpu.SemaphoreType.DMA((len(pieces) + 2,))],
    )
    return pl.pallas_call(
        assemble_kernel,
        grid_spec=spec,
        out_shape=jax.ShapeDtypeStruct((len(pieces) + 1,) + unit.shape, unit.dtype),
        cost_estimate=cost(0, 4 * (len(pieces) + 1) * unit.size),
    )(order, *pieces, far_a, far_b)


def norm_back_kernel(v_ref, part, recv, skip, gain, dv_out, low_out, sums):
    @pl.when(pl.program_id(0) == 0)
    def _():
        sums[...] = jnp.zeros_like(sums)

    dout = part[...].astype(F32) + recv[...].astype(F32)
    dv, dg, db = norm_back(v_ref[...].astype(F32), dout, gain[...])
    dv = skip[...].astype(F32) + dv
    if dv_out is not None:
        dv_out[...] = dv
    low_out[...] = dv.astype(BF)
    sums[0:1] += dg
    sums[1:2] += db


def through_norm(v, part, recv, skip, gain, keep):
    rows, width = v.shape
    tile = 256
    spec = pl.BlockSpec((tile, width), lambda i: (i, 0))
    kernel = norm_back_kernel if keep else (lambda *r: norm_back_kernel(*r[:5], None, *r[5:]))
    outs = [jax.ShapeDtypeStruct((rows, width), F32)] if keep else []
    return pl.pallas_call(
        kernel,
        grid=(rows // tile,),
        in_specs=[spec] * 4 + [pl.BlockSpec((1, width), lambda i: (0, 0))],
        out_specs=[spec] * (1 + keep) + [pl.BlockSpec((2, width), lambda i: (0, 0))],
        out_shape=outs + [jax.ShapeDtypeStruct((rows, width), BF), jax.ShapeDtypeStruct((2, width), F32)],
        cost_estimate=cost(30 * rows * width, 16 * 2**20),
        **params(32),
    )(v, part, recv, skip, gain)


def head_grad_kernel(core, da, db, oa, ob, w, do_out, gw_out, acc):
    step = pl.program_id(0)
    steps = pl.num_programs(0)
    d = jnp.where(step < steps // 2, da[...], db[...])
    weight = w[...].reshape(w.shape[0] * w.shape[1], w.shape[2])
    do_out[...] = mm(d, weight, NN).astype(BF)

    @pl.when(step == 0)
    def _():
        acc[...] = jnp.zeros_like(acc)

    acc[...] += mm(d, jnp.concatenate([oa[...], ob[...]], axis=1), TN)

    @pl.when(step == steps - 1)
    def _():
        gw_out[...] = acc[...].astype(BF)


def head_grad(core, d_own, d_oth, mixed, g1):
    rows, width = d_own.shape
    tile = 512
    half = rows // tile
    chips, per, _ = g1.shape
    spec = pltpu.PrefetchScalarGridSpec(
        num_scalar_prefetch=1,
        grid=(2 * half,),
        in_specs=[
            pl.BlockSpec((tile, width), lambda i, c: (jnp.minimum(i, half - 1), 0)),
            pl.BlockSpec((tile, width), lambda i, c: (jnp.maximum(i - half, 0), 0)),
            pl.BlockSpec((tile, 256), lambda i, c: (i % half + half * ((i // half) ^ c[0]), 0)),
            pl.BlockSpec((tile, 256), lambda i, c: (i % half + half * ((i // half) ^ c[0]), 0)),
            pl.BlockSpec((chips, per, 512), lambda i, c: (0, 0, 3)),
        ],
        out_specs=[
            pl.BlockSpec((tile, 512), lambda i, c: (i % half + half * ((i // half) ^ c[0]), 0)),
            pl.BlockSpec((width, 512), lambda i, c: (0, 0)),
        ],
        scratch_shapes=[pltpu.VMEM((width, 512), F32)],
    )
    return pl.pallas_call(
        head_grad_kernel,
        grid_spec=spec,
        out_shape=[
            jax.ShapeDtypeStruct((2 * rows, 512), BF),
            jax.ShapeDtypeStruct((width, 512), BF),
        ],
        cost_estimate=cost(8 * rows * width * 512, 12 * 2**20),
        **params(48),
    )(core, d_own, d_oth, *mixed, g1)


def project_weight_kernel(a1, *refs):
    *grads, gw_out, acc = refs
    step = pl.program_id(0)
    grad = jnp.concatenate([g[...] for g in grads], axis=1)

    @pl.when(step == 0)
    def _():
        acc[...] = jnp.zeros_like(acc)

    acc[...] += mm(a1[...], grad, TN)

    @pl.when(step == pl.num_programs(0) - 1)
    def _():
        gw_out[...] = acc[...].astype(BF)


def project_weight(a1, grads):
    rows2, width = a1.shape
    tile = 512
    wide = sum(g.shape[1] for g in grads)
    return pl.pallas_call(
        project_weight_kernel,
        grid=(rows2 // tile,),
        in_specs=[pl.BlockSpec((tile, width), lambda i: (i, 0))]
        + [pl.BlockSpec((tile, g.shape[1]), lambda i: (i, 0)) for g in grads],
        out_specs=pl.BlockSpec((width, wide), lambda i: (0, 0)),
        scratch_shapes=[pltpu.VMEM((width, wide), F32)],
        out_shape=jax.ShapeDtypeStruct((width, wide), BF),
        cost_estimate=cost(2 * rows2 * width * wide, 14 * 2**20),
        **params(56),
    )(a1, *grads)


def project_back_kernel(core, *refs):
    *grads, w, d_oth, d_own = refs
    step = pl.program_id(0)
    steps = pl.num_programs(0)
    grad = jnp.concatenate([g[...] for g in grads], axis=1)
    weight = w[...].reshape(w.shape[0] * w.shape[1], w.shape[2])
    part = mm(grad, weight, NT)

    @pl.when(step < steps // 2)
    def _():
        d_oth[...] = part.astype(BF)

    @pl.when(step >= steps // 2)
    def _():
        d_own[...] = part


def project_back(core, grads, g1):
    rows = grads[0].shape[0] // 2
    chips, per, _ = g1.shape
    width = chips * per
    tile = 512
    half = rows // tile
    wide = sum(g.shape[1] for g in grads)

    def place(i, c):
        return (i % half + half * (1 - (i // half) ^ c[0]), 0)

    spec = pltpu.PrefetchScalarGridSpec(
        num_scalar_prefetch=1,
        grid=(2 * half,),
        in_specs=[pl.BlockSpec((tile, g.shape[1]), place) for g in grads]
        + [pl.BlockSpec((chips, per, wide), lambda i, c: (0, 0, 0))],
        out_specs=[
            pl.BlockSpec((tile, width), lambda i, c: (jnp.minimum(i, half - 1), 0)),
            pl.BlockSpec((tile, width), lambda i, c: (jnp.maximum(i - half, 0), 0)),
        ],
    )
    return pl.pallas_call(
        project_back_kernel,
        grid_spec=spec,
        out_shape=[
            jax.ShapeDtypeStruct((rows, width), BF),
            jax.ShapeDtypeStruct((rows, width), F32),
        ],
        cost_estimate=cost(4 * rows * width * wide, 16 * 2**20),
        **params(56),
    )(core, *grads, g1)


def fast_shards(tokens, segment_ids, w_qkv, w_out, w_in, w_back, norm_gains, norm_biases, cotangent):
    both = ("chip", "core", "tensor")
    alike = ("chip", "tensor")
    chip, core, y = [lax.axis_index(n) for n in both]
    chips = lax.axis_size("chip")
    dp_rank = chip * 2 + core
    far = chips // 2
    at_home = core == y

    def ident(q, k, j):
        return (q * 2 + k) * 2 + j

    cells = [(q, k, j) for q in range(chips) for k in range(2) for j in range(2)]
    place_of = {q: p for p, q in enumerate(RING)}
    to_core = [(ident(q, k, j), ident(q, 1 - k, j)) for q, k, j in cells]
    to_y = [(ident(q, k, j), ident(q, k, 1 - j)) for q, k, j in cells]
    diagonal = [(ident(q, k, j), ident(q, j, k)) for q, k, j in cells]
    back = [(ident(q, k, j), ident(q, j, k)) for q, k, j in cells if k != j]
    turn = {d: [(ident(q, k, j), ident(RING[(place_of[q] + d) % chips], k, j)) for q, k, j in cells] for d in (1, -1)}
    hops = [[(ident(q, k, j), ident(q ^ m, k, j)) for q, k, j in cells] for m in (1, 2, 4)]
    near = [0] + [s * d for d in range(1, far) for s in (-1, 1)] + [far]
    table = jnp.array([[RING[(place_of[q] + d) % chips] for d in near] for q in range(chips)], jnp.int32)
    where = lax.dynamic_index_in_dim(table, chip, 0, keepdims=False)

    def chip_at(d):
        return where[near.index(d if d != -far else far)]

    def send(v, pairs):
        return lax.ppermute(v, both, pairs)

    class Gather:
        def __init__(self, unit):
            self.got = {0: unit}
            self.half = unit.shape[0] // 2

        def step(self, n, *deps):
            right, left = after((self.got[1 - n], self.got[n - 1]), *deps)
            if n == far:
                right, left = right[: self.half], left[self.half :]
            self.got[-n], self.got[n] = send(right, turn[1]), send(left, turn[-1])
            return right, left

        def whole(self):
            return assemble(where, [self.got[d] for d in near[:-1]], self.got[-far], self.got[far])

    class Reduce:
        def __init__(self, blocks):
            self.blocks = blocks
            self.half = blocks.shape[1] // 2
            self.got = None

        def block(self, d):
            return lax.dynamic_index_in_dim(self.blocks, chip_at(d), 0, keepdims=False)

        def step(self, n, *deps):
            half = self.half
            if n == 1:
                whole = self.block(far)
                pieces = after((whole[:half], whole[half:]), *deps)
            else:
                pieces = []
                for way, got in zip((1, -1), after(tuple(self.got), *deps)):
                    mine = self.block(way * (far - n + 1))
                    if n == 2:
                        pad = ((0, half), (0, 0)) if way == 1 else ((half, 0), (0, 0))
                        got = jnp.pad(got, pad)
                    pieces.append((mine.astype(F32) + got.astype(F32)).astype(BF))
            self.got = send(pieces[0], turn[1]), send(pieces[1], turn[-1])
            return tuple(pieces)

        def total(self):
            return self.block(0).astype(F32) + self.got[0].astype(F32) + self.got[1].astype(F32)

    def to_owner(total):
        per = total.shape[0] // 2
        mine = lax.dynamic_slice_in_dim(total, core * per, per, 0)
        theirs = lax.dynamic_slice_in_dim(total, (1 - core) * per, per, 0).astype(BF)
        recv = send(theirs, to_core).astype(F32)
        keep = jnp.where(at_home, mine, recv)
        leave = jnp.where(at_home, recv, mine).astype(BF)
        return keep + send(leave, to_y).astype(F32)

    def unit_of(own, across):
        mine = jnp.where(at_home, own, across)
        recv = send(jnp.where(at_home, across, own), to_core)
        return jnp.where(core == 0, jnp.concatenate([mine, recv]), jnp.concatenate([recv, mine]))

    width = tokens.shape[2]
    core_arg = core.astype(jnp.int32)[None]
    heads = w_qkv.shape[2] // HEAD
    slopes = jnp.exp2(-(core * heads + jnp.arange(heads, dtype=jnp.int32) + 1).astype(F32)) * LOG2E

    def reduce_chips(blocks):
        return lax.psum_scatter(blocks.reshape(width, -1), "chip", scatter_dimension=0, tiled=True)

    pad = jnp.zeros((norm_gains.shape[1], 124), F32)
    shard1 = jnp.concatenate(
        [w_qkv[0], w_qkv[1], w_qkv[2], w_out.T, norm_gains.T, norm_biases.T, pad], axis=1
    ).astype(BF)
    low_in = w_in.astype(BF)
    low_back = w_back.T.astype(BF)
    cross1 = send(shard1, to_y)
    seg = jnp.where(at_home, segment_ids, send(segment_ids, to_core))
    seg_col = seg.reshape(-1, 1)
    g1 = Gather(unit_of(shard1, cross1))
    sent = g1.step(1)
    cross2 = send(after(low_in, cross1), to_y)
    cross_x = send(after(tokens[0], cross2), back)
    sent = g1.step(2, cross2)
    sent = g1.step(3)
    sent = g1.step(4, cross_x)
    x_own = jnp.where(at_home, tokens[0], after(cross_x, *sent))
    x_oth = send(x_own, to_core)
    g2 = Gather(unit_of(low_in, after(cross2, *sent)))
    sent = g2.step(1, g1.got[-far], g1.got[far])
    cross_y = send(after(cotangent[0], *sent), back)
    wa = g1.whole()
    wide = 4 * heads * HEAD
    gb = wa[:, :, wide : wide + 4].reshape(width, 4).astype(F32).T

    a1, qkv = project(core_arg, after(x_own, *sent), x_oth, gb, wa)
    sent = g2.step(2, qkv)
    mixed0, logs0 = attend(slopes, after(qkv, *sent, cross_y), seg_col, 0, 2)
    sent = g2.step(3, mixed0)
    w2 = lax.all_gather(after(low_back, *sent), both)
    w2 = w2.reshape(2 * chips, 2, *w2.shape[1:])
    mixed1, logs1 = attend(slopes, after(qkv, *sent), seg_col, 2, 2)
    y_own = jnp.where(at_home, cotangent[0], after(cross_y, mixed1))
    y_oth = send(y_own, to_core)
    sent = g2.step(4, mixed1)
    mixed = (after(mixed0, *sent, y_own), mixed1)
    part_oth, part_own = branch(core_arg, mixed, wa, x_own)
    h1, a2_own = residual(part_own, send(part_oth, to_core), gb)
    a2_oth = send(a2_own, to_core)
    w1 = g2.whole()
    hidden, slope, gw2 = up(core_arg, a2_own, a2_oth, y_own, y_oth, w1)
    r2 = reduce_chips(gw2)
    f_own, f_oth, d_own, d_oth, gw1 = down(core_arg, a2_own, a2_oth, after(y_own, gw2), y_oth, hidden, slope, w1, w2)
    r1 = reduce_chips(gw1)
    d_recv = send(d_oth, to_core)
    dh1, da_own, sums2 = through_norm(h1, d_own, d_recv, y_own, gb[1:2], True)
    da_oth = send(da_own, to_core)
    f_recv = send(after(f_oth, da_own), to_core)
    do, gwo = head_grad(core_arg, da_own, da_oth, mixed, wa)
    result = (h1 + f_own.astype(F32) + after(f_recv, do).astype(F32)).astype(BF)
    cross_result = send(result, back)
    both_mixed = jnp.concatenate(mixed, axis=1)
    both_logs = jnp.concatenate([logs0, logs1], axis=0)
    grads = attend_back(slopes, after(qkv, do, result), do, both_mixed, both_logs, seg)
    result = jnp.where(at_home, result, after(cross_result, grads[0]))
    gwq = project_weight(after(a1, result), grads)
    rc = Reduce(jnp.concatenate([gwq, gwo], axis=1).reshape(chips, width // chips, -1))
    sent = rc.step(1)
    d1_oth, d1_own = project_back(core_arg, after(tuple(grads), *sent), wa)
    d1_recv = send(d1_oth, to_core)
    sent = rc.step(2, d1_own)
    grad_tokens, sums1 = through_norm(x_own, after(d1_own, *sent), d1_recv, dh1, gb[0:1], False)
    cross_tokens = send(grad_tokens, back)
    sent = rc.step(3, sums1)
    sent = rc.step(4, cross_tokens)
    sums = jnp.concatenate([sums1[0:1], sums2[0:1], sums1[1:2], sums2[1:2]], axis=0)
    for pairs in (to_core, to_y, *hops):
        sums = sums + send(sums, pairs)
    grad_back = to_owner(after(r2, sums1).astype(F32))
    grad_in = to_owner(after(r1, *sent).astype(F32))
    r3 = to_owner(rc.total())
    grad_tokens = jnp.where(at_home, grad_tokens, cross_tokens)
    per = r3.shape[0]
    wide = 3 * heads * HEAD
    grad_qkv = r3[:, :wide].reshape(per, 3, -1).transpose(1, 0, 2)
    grad_out = r3[:, wide:].T
    sums = lax.dynamic_slice_in_dim(sums, dp_rank * norm_gains.shape[1], norm_gains.shape[1], 1)
    return (result[None], grad_tokens[None], grad_qkv, grad_out, grad_in, grad_back.T, sums[0:2], sums[2:4])


def solution(mesh):
    n_dp, n_tensor = mesh.shape["dp"], mesh.shape["tensor"]
    if n_dp == 16 and n_tensor == 2:
        grid = Mesh(mesh.devices.reshape(n_dp // 2, 2, n_tensor), ("chip", "core", "tensor"))
        body, dp = fast_shards, ("chip", "core")
    else:
        grid, body, dp = mesh, shards, "dp"
    return jax.shard_map(
        body,
        mesh=grid,
        in_specs=(
            P(dp, "tensor", None),
            P(dp, None),
            P(None, dp, "tensor"),
            P("tensor", dp),
            P(dp, "tensor"),
            P("tensor", dp),
            P(None, dp),
            P(None, dp),
            P(dp, "tensor", None),
        ),
        out_specs=(
            P(dp, "tensor", None),
            P(dp, "tensor", None),
            P(None, dp, "tensor"),
            P("tensor", dp),
            P(dp, "tensor"),
            P("tensor", dp),
            P(None, dp),
            P(None, dp),
        ),
        check_vma=False,
    )
```

```python
import math

import jax
import jax.numpy as jnp
from jax import lax
from jax.experimental import pallas as pl
from jax.experimental.pallas import tpu as pltpu
from jax.sharding import Mesh
from jax.sharding import PartitionSpec as P

HEAD = 128
ROW_BLOCK = 512


eps_norm = 1e-05
masked_score = -1e30


def layer_norm(values, gain, shift):
    center = values - jnp.mean(values, axis=-1, keepdims=True)
    spread = jnp.mean(center * center, axis=-1, keepdims=True)
    return center * lax.rsqrt(spread + eps_norm) * gain + shift


def smooth_act(values):
    return jax.nn.gelu(values, approximate=True)


def block_scores(query_rows, keys, seg_rows, seg_all, row_ids, slopes):
    scale = 1.0 / math.sqrt(HEAD)
    raw = jnp.einsum("qhd,khd->hqk", query_rows, keys, preferred_element_type=jnp.float32) * scale
    cols = jnp.arange(keys.shape[0], dtype=jnp.int32)
    dist = (row_ids[:, None] - cols[None, :]).astype(jnp.float32)
    raw = raw - slopes[:, None, None] * dist[None]
    allowed = (cols[None, :] <= row_ids[:, None]) & (seg_rows[:, None] == seg_all[None, :])
    return jnp.where(allowed[None], raw, masked_score)


def attend_forward(qkv_seq, seg_seq, slopes):
    query, keys, values = (qkv_seq[0], qkv_seq[1], qkv_seq[2])
    length = keys.shape[0]

    def one_block(start):
        rows = lax.dynamic_slice_in_dim(query, start, ROW_BLOCK, 0)
        seg_rows = lax.dynamic_slice_in_dim(seg_seq, start, ROW_BLOCK, 0)
        row_ids = start + jnp.arange(ROW_BLOCK, dtype=jnp.int32)
        scores = block_scores(rows, keys, seg_rows, seg_seq, row_ids, slopes)
        top = jnp.max(scores, axis=-1, keepdims=True)
        expo = jnp.exp(scores - top)
        total = jnp.sum(expo, axis=-1, keepdims=True)
        probs = (expo / total).astype(jnp.bfloat16)
        mixed = jnp.einsum("hqk,khd->qhd", probs, values, preferred_element_type=jnp.float32)
        return (mixed, (top + jnp.log(total))[..., 0])

    starts = jnp.arange(length // ROW_BLOCK, dtype=jnp.int32) * ROW_BLOCK
    mixed, log_totals = lax.map(one_block, starts)
    return (mixed.reshape(length, -1), log_totals)


def attend_backward(qkv_seq, seg_seq, log_totals, grad_mixed, slopes):
    query, keys, values = (qkv_seq[0], qkv_seq[1], qkv_seq[2])
    length, heads_here, head_size = keys.shape
    scale = 1.0 / math.sqrt(HEAD)
    grad_rows_all = grad_mixed.reshape(length, heads_here, head_size)

    def one_block(carry, item):
        start, block_totals = item
        rows = lax.dynamic_slice_in_dim(query, start, ROW_BLOCK, 0)
        seg_rows = lax.dynamic_slice_in_dim(seg_seq, start, ROW_BLOCK, 0)
        grad_rows = lax.dynamic_slice_in_dim(grad_rows_all, start, ROW_BLOCK, 0)
        row_ids = start + jnp.arange(ROW_BLOCK, dtype=jnp.int32)
        scores = block_scores(rows, keys, seg_rows, seg_seq, row_ids, slopes)
        probs = jnp.exp(scores - block_totals[..., None])
        grad_probs = jnp.einsum(
            "qhd,khd->hqk", grad_rows, values, preferred_element_type=jnp.float32
        )
        inner = jnp.sum(probs * grad_probs, axis=-1, keepdims=True)
        grad_scores = (probs * (grad_probs - inner)).astype(jnp.bfloat16)
        grad_query = (
            jnp.einsum("hqk,khd->qhd", grad_scores, keys, preferred_element_type=jnp.float32)
            * scale
        )
        grad_keys = (
            carry[0]
            + jnp.einsum("hqk,qhd->khd", grad_scores, rows, preferred_element_type=jnp.float32)
            * scale
        )
        grad_values = carry[1] + jnp.einsum(
            "hqk,qhd->khd",
            probs.astype(jnp.bfloat16),
            grad_rows,
            preferred_element_type=jnp.float32,
        )
        return ((grad_keys, grad_values), grad_query)

    empty = jnp.zeros((length, heads_here, head_size), jnp.float32)
    starts = jnp.arange(length // ROW_BLOCK, dtype=jnp.int32) * ROW_BLOCK
    (grad_keys, grad_values), grad_query = lax.scan(one_block, (empty, empty), (starts, log_totals))
    return jnp.stack([grad_query.reshape(length, heads_here, head_size), grad_keys, grad_values])


def shards(tokens, segment_ids, w_qkv, w_out, w_in, w_back, norm_gains, norm_biases, cotangent):
    low_copies = (
        w_qkv.astype(jnp.bfloat16),
        w_out.astype(jnp.bfloat16),
        w_in.astype(jnp.bfloat16),
        w_back.astype(jnp.bfloat16),
        norm_gains.astype(jnp.bfloat16),
        norm_biases.astype(jnp.bfloat16),
    )
    (
        complete_query_key_value,
        complete_out_weight,
        complete_in_weight,
        complete_back_weight,
        gains_low,
        shifts_low,
    ) = (
        lax.all_gather(low_copies[0], "dp", axis=1, tiled=True),
        lax.all_gather(low_copies[1], "dp", axis=1, tiled=True),
        lax.all_gather(low_copies[2], "dp", axis=0, tiled=True),
        lax.all_gather(low_copies[3], "dp", axis=1, tiled=True),
        lax.all_gather(low_copies[4], "dp", axis=1, tiled=True),
        lax.all_gather(low_copies[5], "dp", axis=1, tiled=True),
    )
    gains = gains_low.astype(jnp.float32)
    shifts = shifts_low.astype(jnp.float32)
    seqs, own_len, width = tokens.shape
    length = segment_ids.shape[1]
    local_width = complete_query_key_value.shape[2]
    heads_here = local_width // HEAD
    rank = lax.axis_index("tensor")
    first_row = rank * own_len
    slopes = jnp.exp2(
        -(rank * heads_here + jnp.arange(heads_here, dtype=jnp.int32) + 1).astype(jnp.float32)
    )
    tokens_f = tokens.astype(jnp.float32)
    tokens_all = lax.all_gather(tokens, "tensor", axis=1, tiled=True).astype(jnp.float32)
    first_normalized = layer_norm(tokens_all, gains[0], shifts[0]).astype(jnp.bfloat16)
    projected = jnp.einsum(
        "gqu,fuk->gfqk",
        first_normalized,
        complete_query_key_value,
        preferred_element_type=jnp.float32,
    ).astype(jnp.bfloat16)
    qkv_heads = projected.reshape(seqs, 3, length, heads_here, HEAD)

    def forward_seq(item):
        return attend_forward(item[0], item[1], slopes)

    mixed, log_totals = lax.map(forward_seq, (qkv_heads, segment_ids))
    attended_values = mixed.astype(jnp.bfloat16)
    attention_slice = jnp.einsum(
        "oin,nh->oih", attended_values, complete_out_weight, preferred_element_type=jnp.float32
    )
    attn_all = lax.psum(attention_slice.astype(jnp.bfloat16), "tensor").astype(jnp.float32)
    resid_all = tokens_all + attn_all
    second_normalized = layer_norm(resid_all, gains[1], shifts[1]).astype(jnp.bfloat16)
    resid = lax.dynamic_slice_in_dim(resid_all, first_row, own_len, 1)
    hidden_preactivation = jnp.einsum(
        "rhi,ip->rhp", second_normalized, complete_in_weight, preferred_element_type=jnp.float32
    )
    hidden_activations = smooth_act(hidden_preactivation).astype(jnp.bfloat16)
    feedforward_slice = jnp.einsum(
        "cow,wv->cov", hidden_activations, complete_back_weight, preferred_element_type=jnp.float32
    )
    ffn_own = lax.psum_scatter(
        feedforward_slice.astype(jnp.bfloat16), "tensor", scatter_dimension=1, tiled=True
    ).astype(jnp.float32)
    result = (resid + ffn_own).astype(jnp.bfloat16)
    cotangent_gathered = lax.all_gather(cotangent, "tensor", axis=1, tiled=True)
    back_weight_gradient_shard = jnp.einsum(
        "ine,inb->eb", hidden_activations, cotangent_gathered, preferred_element_type=jnp.float32
    )
    hidden_gradient = jnp.einsum(
        "jrx,gx->jrg", cotangent_gathered, complete_back_weight, preferred_element_type=jnp.float32
    )
    _, act_pull = jax.vjp(smooth_act, hidden_preactivation)
    preactivation_gradient = act_pull(hidden_gradient)[0].astype(jnp.bfloat16)
    in_weight_gradient_shard = jnp.einsum(
        "bkw,bkz->wz", second_normalized, preactivation_gradient, preferred_element_type=jnp.float32
    )
    second_norm_slice = jnp.einsum(
        "kyj,tj->kyt",
        preactivation_gradient,
        complete_in_weight,
        preferred_element_type=jnp.float32,
    )
    grad_norm2 = lax.psum_scatter(
        second_norm_slice.astype(jnp.bfloat16), "tensor", scatter_dimension=1, tiled=True
    ).astype(jnp.float32)
    _, second_pull = jax.vjp(layer_norm, resid, gains[1], shifts[1])
    grad_resid_norm, grad_gain2, grad_shift2 = second_pull(grad_norm2)
    grad_resid = cotangent.astype(jnp.float32) + grad_resid_norm
    attention_gradient_gathered = lax.all_gather(
        grad_resid.astype(jnp.bfloat16), "tensor", axis=1, tiled=True
    )
    grad_out_local = jnp.einsum(
        "xwq,xwr->qr",
        attended_values,
        attention_gradient_gathered,
        preferred_element_type=jnp.float32,
    )
    grad_attended = jnp.einsum(
        "wik,jk->wij",
        attention_gradient_gathered,
        complete_out_weight,
        preferred_element_type=jnp.float32,
    ).astype(jnp.bfloat16)

    def backward_seq(item):
        return attend_backward(item[0], item[1], item[2], item[3], slopes)

    grad_heads = lax.map(backward_seq, (qkv_heads, segment_ids, log_totals, grad_attended))
    projection_gradient = grad_heads.reshape(seqs, 3, length, local_width).astype(jnp.bfloat16)
    grad_qkv_local = jnp.einsum(
        "phb,pthw->tbw", first_normalized, projection_gradient, preferred_element_type=jnp.float32
    )
    norm1_part = jnp.einsum(
        "zjyw,juw->zyu",
        projection_gradient,
        complete_query_key_value,
        preferred_element_type=jnp.float32,
    )
    grad_norm1 = lax.psum_scatter(
        norm1_part.astype(jnp.bfloat16), "tensor", scatter_dimension=1, tiled=True
    ).astype(jnp.float32)
    _, first_pull = jax.vjp(layer_norm, tokens_f, gains[0], shifts[0])
    grad_tok_norm, grad_gain1, grad_shift1 = first_pull(grad_norm1)
    grad_tokens = (grad_resid + grad_tok_norm).astype(jnp.bfloat16)
    gain_terms = jnp.stack([grad_gain1, grad_gain2])
    shift_terms = jnp.stack([grad_shift1, grad_shift2])
    gain_sum, shift_sum = lax.psum((gain_terms, shift_terms), "tensor")
    summed = (
        lax.psum_scatter(
            grad_qkv_local.astype(jnp.bfloat16), "dp", scatter_dimension=1, tiled=True
        ).astype(jnp.float32),
        lax.psum_scatter(
            grad_out_local.astype(jnp.bfloat16), "dp", scatter_dimension=1, tiled=True
        ).astype(jnp.float32),
        lax.psum_scatter(
            in_weight_gradient_shard.astype(jnp.bfloat16), "dp", scatter_dimension=0, tiled=True
        ).astype(jnp.float32),
        lax.psum_scatter(
            back_weight_gradient_shard.astype(jnp.bfloat16), "dp", scatter_dimension=1, tiled=True
        ).astype(jnp.float32),
        lax.psum_scatter(
            gain_sum.astype(jnp.bfloat16), "dp", scatter_dimension=1, tiled=True
        ).astype(jnp.float32),
        lax.psum_scatter(
            shift_sum.astype(jnp.bfloat16), "dp", scatter_dimension=1, tiled=True
        ).astype(jnp.float32),
    )
    return (result, grad_tokens, summed[0], summed[1], summed[2], summed[3], summed[4], summed[5])


LOG2E = math.log2(math.e)
SCALE2 = LOG2E / math.sqrt(HEAD)
BLK = 512
BF = jnp.bfloat16
F32 = jnp.float32
NN = (((1,), (0,)), ((), ()))
NT = (((1,), (1,)), ((), ()))
TN = (((0,), (0,)), ((), ()))
RING = (0, 2, 4, 6, 7, 5, 3, 1)


def mm(a, b, dims):
    return lax.dot_general(a, b, dims, preferred_element_type=F32)


def params(mib, cost=None):
    return dict(compiler_params=pltpu.CompilerParams(vmem_limit_bytes=mib * 2**20))


def after(v, *deps):
    return lax.optimization_barrier((v,) + deps)[0]


def cost(flops, nbytes, trans=0):
    return pl.CostEstimate(flops=1024, bytes_accessed=1024, transcendentals=0)


def normalize(v):
    c = v - jnp.mean(v, axis=-1, keepdims=True)
    r = lax.rsqrt(jnp.mean(c * c, axis=-1, keepdims=True) + eps_norm)
    return c * r, r


def norm_back(v, dout, gain):
    cn, r = normalize(v)
    t = dout * gain
    dv = r * (t - jnp.mean(t, axis=-1, keepdims=True) - cn * jnp.mean(t * cn, axis=-1, keepdims=True))
    return dv, jnp.sum(dout * cn, axis=0, keepdims=True), jnp.sum(dout, axis=0, keepdims=True)


def project_kernel(core, xa, xb, gb, w, a1_out, qkv_out):
    step = pl.program_id(0)
    half = pl.num_programs(0) // 2
    x = jnp.where(step < half, xa[...], xb[...]).astype(F32)
    a1 = (normalize(x)[0] * gb[0:1] + gb[2:3]).astype(BF)
    a1_out[...] = a1
    weight = w[...].reshape(w.shape[0] * w.shape[1], w.shape[2])
    qkv_out[...] = mm(a1, weight, NN).astype(BF)


def project(core, x_own, x_oth, gb, g1):
    rows, width = x_own.shape
    tile = 512
    half = rows // tile
    chips, per, _ = g1.shape
    wide = 3 * 512
    spec = pltpu.PrefetchScalarGridSpec(
        num_scalar_prefetch=1,
        grid=(2 * half,),
        in_specs=[
            pl.BlockSpec((tile, width), lambda i, c: (jnp.minimum(i, half - 1), 0)),
            pl.BlockSpec((tile, width), lambda i, c: (jnp.maximum(i - half, 0), 0)),
            pl.BlockSpec((4, width), lambda i, c: (0, 0)),
            pl.BlockSpec((chips, per, wide), lambda i, c: (0, 0, 0)),
        ],
        out_specs=[
            pl.BlockSpec((tile, width), lambda i, c: (i % half + half * ((i // half) ^ c[0]), 0)),
            pl.BlockSpec((tile, wide), lambda i, c: (i % half + half * ((i // half) ^ c[0]), 0)),
        ],
    )
    return pl.pallas_call(
        project_kernel,
        grid_spec=spec,
        out_shape=[
            jax.ShapeDtypeStruct((2 * rows, width), BF),
            jax.ShapeDtypeStruct((2 * rows, wide), BF),
        ],
        cost_estimate=cost(4 * rows * width * wide, 12 * 2**20),
        **params(48),
    )(core, x_own, x_oth, gb, g1)


def attend_kernel(slopes, q_ref, k_ref, v_ref, seg_ref, o_ref, l_ref, s_ref):
    m2 = slopes[pl.program_id(0)]
    blocks = q_ref.shape[0] // BLK
    lane = lax.broadcasted_iota(jnp.int32, (1, BLK), 1)
    row = lax.broadcasted_iota(jnp.int32, (BLK, 1), 0)
    for i in range(blocks):
        q = q_ref[i * BLK : (i + 1) * BLK, :]
        seg = seg_ref[i * BLK : (i + 1) * BLK, :]
        top = jnp.full((BLK, 128), masked_score, F32)
        for j in range(i + 1):
            cols = slice(j * BLK, (j + 1) * BLK)
            bias = m2 * (lane + (j - i) * BLK).astype(F32)
            s = mm(q, k_ref[cols, :], NT) * SCALE2 + bias
            allowed = (lane + j * BLK) >= seg
            if j == i:
                allowed = allowed & (lane <= row)
            s = jnp.where(allowed, s, masked_score)
            s_ref[:, cols] = s
            for c in range(0, BLK, 128):
                top = jnp.maximum(top, s[:, c : c + 128])
        top = jnp.max(top, axis=1, keepdims=True)
        total = jnp.zeros((BLK, 128), F32)
        mixed = jnp.zeros((BLK, HEAD), F32)
        for j in range(i + 1):
            cols = slice(j * BLK, (j + 1) * BLK)
            p = jnp.exp2(s_ref[:, cols] - top)
            for c in range(0, BLK, 128):
                total = total + p[:, c : c + 128]
            mixed = mixed + mm(p.astype(BF), v_ref[cols, :], NN)
        total = jnp.sum(total, axis=1, keepdims=True)
        o_ref[i * BLK : (i + 1) * BLK, :] = (mixed / total).astype(BF)
        logs = jnp.broadcast_to(top + jnp.log2(total), (BLK, 128))
        l_ref[0, :, i * BLK : (i + 1) * BLK] = logs.T[0:1, :]


def attend(slopes, qkv, seg_col, first, count):
    length = qkv.shape[0]
    heads = qkv.shape[1] // (3 * HEAD)
    spec = pltpu.PrefetchScalarGridSpec(
        num_scalar_prefetch=1,
        grid=(count,),
        in_specs=[
            pl.BlockSpec((length, HEAD), lambda h, s: (0, first + h)),
            pl.BlockSpec((length, HEAD), lambda h, s: (0, heads + first + h)),
            pl.BlockSpec((length, HEAD), lambda h, s: (0, 2 * heads + first + h)),
            pl.BlockSpec((length, 1), lambda h, s: (0, 0)),
        ],
        out_specs=[
            pl.BlockSpec((length, HEAD), lambda h, s: (0, h)),
            pl.BlockSpec((1, 1, length), lambda h, s: (h, 0, 0)),
        ],
        scratch_shapes=[pltpu.VMEM((BLK, length), F32)],
    )
    return pl.pallas_call(
        attend_kernel,
        grid_spec=spec,
        out_shape=[
            jax.ShapeDtypeStruct((length, count * HEAD), BF),
            jax.ShapeDtypeStruct((count, 1, length), F32),
        ],
        cost_estimate=cost(count * 4 * length * length * HEAD, 3 * count * 2**20, count * length * length),
        **params(48),
    )(lax.slice_in_dim(slopes, first, first + count), qkv, qkv, qkv, seg_col)


def attend_back_kernel(slopes, q_ref, k_ref, v_ref, do_ref, o_ref, l_ref, seg_ref, dq_ref, dk_ref, dv_ref, acc, inner):
    m2 = slopes[pl.program_id(0)]
    blocks = q_ref.shape[0] // BLK
    lane = lax.broadcasted_iota(jnp.int32, (1, BLK), 1)
    row = lax.broadcasted_iota(jnp.int32, (BLK, 1), 0)
    for i in range(blocks):
        rows = slice(i * BLK, (i + 1) * BLK)
        d = jnp.sum(do_ref[rows, :].astype(F32) * o_ref[rows, :].astype(F32), axis=1, keepdims=True)
        inner[:, rows] = jnp.broadcast_to(d, (BLK, 128)).T[0:8, :]
    for j in range(blocks):
        cols = slice(j * BLK, (j + 1) * BLK)
        kj, vj = k_ref[cols, :], v_ref[cols, :]
        dk = jnp.zeros((BLK, HEAD), F32)
        dv = jnp.zeros((BLK, HEAD), F32)
        for i in range(j, blocks):
            rows = slice(i * BLK, (i + 1) * BLK)
            qi, doi = q_ref[rows, :], do_ref[rows, :]
            bias = m2 * (row + (j - i) * BLK).astype(F32)
            s = mm(kj, qi, NT) * SCALE2 + bias - l_ref[0, :, rows]
            allowed = (row + j * BLK) >= seg_ref[:, rows]
            if j == i:
                allowed = allowed & (row <= lane)
            p = jnp.exp2(jnp.where(allowed, s, masked_score))
            ds = (p * (mm(vj, doi, NT) - inner[0:1, rows])).astype(BF)
            dv = dv + mm(p.astype(BF), doi, NN)
            dk = dk + mm(ds, qi, NN)
            dq = mm(ds, kj, TN)
            if j == 0:
                acc[rows, :] = dq
            else:
                acc[rows, :] += dq
        dk_ref[cols, :] = (dk * (1.0 / math.sqrt(HEAD))).astype(BF)
        dv_ref[cols, :] = dv.astype(BF)
    dq_ref[...] = (acc[...] * (1.0 / math.sqrt(HEAD))).astype(BF)


def attend_back(slopes, qkv, grad, mixed, logs, seg_row):
    length = qkv.shape[0]
    heads = qkv.shape[1] // (3 * HEAD)

    def column(at):
        return pl.BlockSpec((length, HEAD), lambda h, s: (0, at + h))

    spec = pltpu.PrefetchScalarGridSpec(
        num_scalar_prefetch=1,
        grid=(heads,),
        in_specs=[
            column(0),
            column(heads),
            column(2 * heads),
            column(0),
            column(0),
            pl.BlockSpec((1, 1, length), lambda h, s: (h, 0, 0)),
            pl.BlockSpec((1, length), lambda h, s: (0, 0)),
        ],
        out_specs=[column(0)] * 3,
        scratch_shapes=[pltpu.VMEM((length, HEAD), F32), pltpu.VMEM((8, length), F32)],
    )
    return pl.pallas_call(
        attend_back_kernel,
        grid_spec=spec,
        out_shape=[jax.ShapeDtypeStruct((length, heads * HEAD), BF)] * 3,
        cost_estimate=cost(heads * 10 * length * length * HEAD, 5 * heads * 2**20, heads * length * length),
        **params(48),
    )(slopes, qkv, qkv, qkv, grad, mixed, logs, seg_row)


def branch_oth_kernel(core, oa, ob, w, out):
    weight = w[...].reshape(w.shape[0] * w.shape[1], w.shape[2])
    out[...] = mm(jnp.concatenate([oa[...], ob[...]], axis=1), weight, NT).astype(BF)


def branch_own_kernel(core, oa, ob, w, x_ref, out):
    weight = w[...].reshape(w.shape[0] * w.shape[1], w.shape[2])
    out[...] = x_ref[...].astype(F32) + mm(jnp.concatenate([oa[...], ob[...]], axis=1), weight, NT)


def branch(core, mixed, weights, x_own=None):
    rows = mixed[0].shape[0] // 2
    chips, per, _ = weights.shape
    width = chips * per
    tile = 512
    half = rows // tile
    own = x_own is not None
    own_rows = pl.BlockSpec((tile, width), lambda i, c: (i, 0))

    def place(i, c):
        return (i + half * (c[0] if own else 1 - c[0]), 0)

    spec = pltpu.PrefetchScalarGridSpec(
        num_scalar_prefetch=1,
        grid=(half,),
        in_specs=[pl.BlockSpec((tile, 256), place)] * 2
        + [pl.BlockSpec((chips, per, 512), lambda i, c: (0, 0, 3))]
        + ([own_rows] if own else []),
        out_specs=own_rows,
    )
    return pl.pallas_call(
        branch_own_kernel if own else branch_oth_kernel,
        grid_spec=spec,
        out_shape=jax.ShapeDtypeStruct((rows, width), F32 if own else BF),
        cost_estimate=cost(2 * rows * width * 512, 6 * 2**20),
        **params(48),
    )(core, *mixed, weights, *([x_own] if own else []))


def residual_kernel(part, recv, gb, h_out, a2_out):
    h = part[...] + recv[...].astype(F32)
    h_out[...] = h
    a2_out[...] = (normalize(h)[0] * gb[1:2] + gb[3:4]).astype(BF)


def residual(part, recv, gb):
    rows, width = part.shape
    tile = 256
    spec = pl.BlockSpec((tile, width), lambda i: (i, 0))
    return pl.pallas_call(
        residual_kernel,
        grid=(rows // tile,),
        in_specs=[spec, spec, pl.BlockSpec((4, width), lambda i: (0, 0))],
        out_specs=[spec, spec],
        out_shape=[
            jax.ShapeDtypeStruct((rows, width), F32),
            jax.ShapeDtypeStruct((rows, width), BF),
        ],
        cost_estimate=cost(20 * rows * width, 12 * 2**20),
        **params(32),
    )(part, recv, gb)


def up_kernel(core, aa, ab, ya, yb, w_ref, g_out, s_out, gw_out, acc):
    step = pl.program_id(0)
    steps = pl.num_programs(0)
    a2 = jnp.where(step < steps // 2, aa[...], ab[...])
    dyt = jnp.where(step < steps // 2, ya[...], yb[...]).T
    chips, per, hidden = w_ref.shape
    chunk = 512
    c0, c1 = math.sqrt(2.0 / math.pi), 0.044715

    @pl.when(step == 0)
    def _():
        acc[...] = jnp.zeros_like(acc)

    def product(c):
        return mm(a2, w_ref[:, :, c : c + chunk].reshape(chips * per, chunk), NN)

    u, held = product(0), []
    for c in range(0, hidden, chunk):
        cols = slice(c, c + chunk)
        later = product(c + chunk) if c + chunk < hidden else None
        sq = u * u
        th = jnp.tanh(u * (c0 + c0 * c1 * sq))
        hp = 0.5 + 0.5 * th
        g = (u * hp).astype(BF)
        g_out[:, cols] = g
        s_out[:, cols] = (hp + (0.5 * u) * (1.0 - th * th) * (c0 + 3.0 * c0 * c1 * sq)).astype(BF)
        held.append((cols, g))
        if c > 0:
            acc[:, held[-2][0]] += mm(dyt, held[-2][1], NN)
        u = later
    acc[:, held[-1][0]] += mm(dyt, held[-1][1], NN)

    @pl.when(step == steps - 1)
    def _():
        gw_out[...] = acc[...].astype(BF).reshape(gw_out.shape)


def halves(tile, width, half):
    return [
        pl.BlockSpec((tile, width), lambda i, *c: (jnp.minimum(i, half - 1), 0)),
        pl.BlockSpec((tile, width), lambda i, *c: (jnp.maximum(i - half, 0), 0)),
    ]


def ringed(w):
    return pl.BlockSpec(w.shape, lambda i, *c: (0, 0, 0), pipeline_mode=pl.Buffered(1))


def gathered(w):
    return pl.BlockSpec((w.shape[0], 1) + w.shape[2:], lambda i, c: (0, c[0], 0, 0), pipeline_mode=pl.Buffered(1))


def up(core, a_own, a_oth, y_own, y_oth, w1):
    rows, width = a_own.shape
    chips, _, hidden = w1.shape
    tile = 512
    out = pl.BlockSpec((tile, hidden), lambda i, c: (i, 0))
    spec = pltpu.PrefetchScalarGridSpec(
        num_scalar_prefetch=1,
        grid=(2 * rows // tile,),
        in_specs=halves(tile, width, rows // tile) * 2 + [ringed(w1)],
        out_specs=[
            out,
            out,
            pl.BlockSpec((chips, width // chips, hidden), lambda i, c: (0, 0, 0), pipeline_mode=pl.Buffered(1)),
        ],
        scratch_shapes=[pltpu.VMEM((width, hidden), F32)],
    )
    return pl.pallas_call(
        up_kernel,
        grid_spec=spec,
        out_shape=[jax.ShapeDtypeStruct((2 * rows, hidden), BF)] * 2
        + [jax.ShapeDtypeStruct((chips, width // chips, hidden), BF)],
        cost_estimate=cost(8 * rows * width * hidden, 32 * 2**20, 2 * rows * hidden),
        **params(60),
    )(core, a_own, a_oth, y_own, y_oth, w1)


def down_kernel(core, aa, ab, ya, yb, g_ref, s_ref, w1_ref, w2_ref, f_own, f_oth, d_own, d_oth, gw_out, a2t_s, du_s):
    step = pl.program_id(0)
    steps = pl.num_programs(0)
    half = steps // 2
    chips, per, hidden = w1_ref.shape
    width = chips * per
    tile = aa.shape[0]
    rows = pl.ds(pl.multiple_of(step * tile, tile), tile)
    a2t_s[:, rows] = jnp.where(step < half, aa[...], ab[...]).T
    dy = jnp.where(step < half, ya[...], yb[...])
    chunk = 512
    for c in range(0, hidden, chunk):
        cols = slice(c, c + chunk)
        dg = mm(dy, w2_ref[:, 0, :, cols].reshape(width, chunk), NN)
        du_s[rows, cols] = (dg * s_ref[:, cols].astype(F32)).astype(BF)
    f = mm(g_ref[...], w2_ref[:, 0].reshape(width, hidden), NT).astype(BF)
    d = mm(du_s[rows, :], w1_ref[...].reshape(width, hidden), NT).astype(BF)

    @pl.when(step < half)
    def _():
        f_own[...] = f
        d_own[...] = d

    @pl.when(step >= half)
    def _():
        f_oth[...] = f
        d_oth[...] = d

    @pl.when(step == steps - 1)
    def _():
        for c in range(0, hidden, chunk):
            cols = slice(c, c + chunk)
            gw_out[:, :, cols] = mm(a2t_s[...], du_s[:, cols], NN).astype(BF).reshape(chips, per, chunk)


def down(core, a_own, a_oth, y_own, y_oth, hidden_units, slope, w1, w2):
    rows, width = a_own.shape
    chips, per, hidden = w1.shape
    tile = 512
    units = pl.BlockSpec((tile, hidden), lambda i, c: (i, 0))
    spec = pltpu.PrefetchScalarGridSpec(
        num_scalar_prefetch=1,
        grid=(2 * rows // tile,),
        in_specs=halves(tile, width, rows // tile) * 2 + [units, units, ringed(w1), gathered(w2)],
        out_specs=halves(tile, width, rows // tile) * 2
        + [pl.BlockSpec((chips, per, hidden), lambda i, c: (0, 0, 0), pipeline_mode=pl.Buffered(1))],
        scratch_shapes=[pltpu.VMEM((width, 2 * rows), BF), pltpu.VMEM((2 * rows, hidden), BF)],
    )
    return pl.pallas_call(
        down_kernel,
        grid_spec=spec,
        out_shape=[jax.ShapeDtypeStruct((rows, width), BF)] * 4
        + [jax.ShapeDtypeStruct((chips, per, hidden), BF)],
        cost_estimate=cost(16 * rows * width * hidden, 40 * 2**20),
        **params(60),
    )(core, a_own, a_oth, y_own, y_oth, hidden_units, slope, w1, w2)


def assemble_kernel(order, *refs):
    *pieces, far_a, far_b, out, sems = refs
    half = far_a.shape[0]
    n = len(pieces)
    copies = [pltpu.make_async_copy(p, out.at[order[i]], sems.at[i]) for i, p in enumerate(pieces)]
    copies.append(pltpu.make_async_copy(far_a, out.at[order[n], pl.ds(0, half)], sems.at[n]))
    copies.append(pltpu.make_async_copy(far_b, out.at[order[n], pl.ds(half, half)], sems.at[n + 1]))
    for c in copies:
        c.start()
    for c in copies:
        c.wait()


def assemble(order, pieces, far_a, far_b):
    unit = pieces[0]
    any_ = pl.BlockSpec(memory_space=pl.ANY)
    spec = pltpu.PrefetchScalarGridSpec(
        num_scalar_prefetch=1,
        grid=(1,),
        in_specs=[pl.BlockSpec(p.shape, lambda i, o: (0, 0)) for p in (*pieces, far_a, far_b)],
        out_specs=any_,
        scratch_shapes=[pltpu.SemaphoreType.DMA((len(pieces) + 2,))],
    )
    return pl.pallas_call(
        assemble_kernel,
        grid_spec=spec,
        out_shape=jax.ShapeDtypeStruct((len(pieces) + 1,) + unit.shape, unit.dtype),
        cost_estimate=cost(0, 4 * (len(pieces) + 1) * unit.size),
    )(order, *pieces, far_a, far_b)


def norm_back_kernel(v_ref, part, recv, skip, gain, dv_out, low_out, sums):
    @pl.when(pl.program_id(0) == 0)
    def _():
        sums[...] = jnp.zeros_like(sums)

    dout = part[...].astype(F32) + recv[...].astype(F32)
    dv, dg, db = norm_back(v_ref[...].astype(F32), dout, gain[...])
    dv = skip[...].astype(F32) + dv
    if dv_out is not None:
        dv_out[...] = dv
    low_out[...] = dv.astype(BF)
    sums[0:1] += dg
    sums[1:2] += db


def through_norm(v, part, recv, skip, gain, keep):
    rows, width = v.shape
    tile = 256
    spec = pl.BlockSpec((tile, width), lambda i: (i, 0))
    kernel = norm_back_kernel if keep else (lambda *r: norm_back_kernel(*r[:5], None, *r[5:]))
    outs = [jax.ShapeDtypeStruct((rows, width), F32)] if keep else []
    return pl.pallas_call(
        kernel,
        grid=(rows // tile,),
        in_specs=[spec] * 4 + [pl.BlockSpec((1, width), lambda i: (0, 0))],
        out_specs=[spec] * (1 + keep) + [pl.BlockSpec((2, width), lambda i: (0, 0))],
        out_shape=outs + [jax.ShapeDtypeStruct((rows, width), BF), jax.ShapeDtypeStruct((2, width), F32)],
        cost_estimate=cost(30 * rows * width, 16 * 2**20),
        **params(32),
    )(v, part, recv, skip, gain)


def head_grad_kernel(core, da, db, oa, ob, w, do_out, gw_out, acc):
    step = pl.program_id(0)
    steps = pl.num_programs(0)
    d = jnp.where(step < steps // 2, da[...], db[...])
    weight = w[...].reshape(w.shape[0] * w.shape[1], w.shape[2])
    do_out[...] = mm(d, weight, NN).astype(BF)

    @pl.when(step == 0)
    def _():
        acc[...] = jnp.zeros_like(acc)

    acc[...] += mm(d, jnp.concatenate([oa[...], ob[...]], axis=1), TN)

    @pl.when(step == steps - 1)
    def _():
        gw_out[...] = acc[...].astype(BF)


def head_grad(core, d_own, d_oth, mixed, g1):
    rows, width = d_own.shape
    tile = 512
    half = rows // tile
    chips, per, _ = g1.shape
    spec = pltpu.PrefetchScalarGridSpec(
        num_scalar_prefetch=1,
        grid=(2 * half,),
        in_specs=[
            pl.BlockSpec((tile, width), lambda i, c: (jnp.minimum(i, half - 1), 0)),
            pl.BlockSpec((tile, width), lambda i, c: (jnp.maximum(i - half, 0), 0)),
            pl.BlockSpec((tile, 256), lambda i, c: (i % half + half * ((i // half) ^ c[0]), 0)),
            pl.BlockSpec((tile, 256), lambda i, c: (i % half + half * ((i // half) ^ c[0]), 0)),
            pl.BlockSpec((chips, per, 512), lambda i, c: (0, 0, 3)),
        ],
        out_specs=[
            pl.BlockSpec((tile, 512), lambda i, c: (i % half + half * ((i // half) ^ c[0]), 0)),
            pl.BlockSpec((width, 512), lambda i, c: (0, 0)),
        ],
        scratch_shapes=[pltpu.VMEM((width, 512), F32)],
    )
    return pl.pallas_call(
        head_grad_kernel,
        grid_spec=spec,
        out_shape=[
            jax.ShapeDtypeStruct((2 * rows, 512), BF),
            jax.ShapeDtypeStruct((width, 512), BF),
        ],
        cost_estimate=cost(8 * rows * width * 512, 12 * 2**20),
        **params(48),
    )(core, d_own, d_oth, *mixed, g1)


def project_weight_kernel(a1, gwo, *refs):
    *grads, gw_out, acc = refs
    step = pl.program_id(0)
    grad = jnp.concatenate([g[...] for g in grads], axis=1)
    wide = grad.shape[1]

    @pl.when(step == 0)
    def _():
        acc[...] = jnp.zeros_like(acc)
        gw_out[:, wide:] = gwo[...]

    acc[...] += mm(a1[...], grad, TN)

    @pl.when(step == pl.num_programs(0) - 1)
    def _():
        gw_out[:, :wide] = acc[...].astype(BF)


def project_weight(a1, gwo, grads):
    rows2, width = a1.shape
    tile = 512
    wide = sum(g.shape[1] for g in grads)
    total = wide + gwo.shape[1]
    return pl.pallas_call(
        project_weight_kernel,
        grid=(rows2 // tile,),
        in_specs=[pl.BlockSpec((tile, width), lambda i: (i, 0)), pl.BlockSpec(gwo.shape, lambda i: (0, 0))]
        + [pl.BlockSpec((tile, g.shape[1]), lambda i: (i, 0)) for g in grads],
        out_specs=pl.BlockSpec((width, total), lambda i: (0, 0)),
        scratch_shapes=[pltpu.VMEM((width, wide), F32)],
        out_shape=jax.ShapeDtypeStruct((width, total), BF),
        cost_estimate=cost(2 * rows2 * width * wide, 14 * 2**20),
        **params(56),
    )(a1, gwo, *grads)


def project_back_kernel(core, *refs):
    *grads, w, d_oth, d_own = refs
    step = pl.program_id(0)
    steps = pl.num_programs(0)
    grad = jnp.concatenate([g[...] for g in grads], axis=1)
    weight = w[...].reshape(w.shape[0] * w.shape[1], w.shape[2])
    part = mm(grad, weight, NT)

    @pl.when(step < steps // 2)
    def _():
        d_oth[...] = part.astype(BF)

    @pl.when(step >= steps // 2)
    def _():
        d_own[...] = part


def project_back(core, grads, g1):
    rows = grads[0].shape[0] // 2
    chips, per, _ = g1.shape
    width = chips * per
    tile = 512
    half = rows // tile
    wide = sum(g.shape[1] for g in grads)

    def place(i, c):
        return (i % half + half * (1 - (i // half) ^ c[0]), 0)

    spec = pltpu.PrefetchScalarGridSpec(
        num_scalar_prefetch=1,
        grid=(2 * half,),
        in_specs=[pl.BlockSpec((tile, g.shape[1]), place) for g in grads]
        + [pl.BlockSpec((chips, per, wide), lambda i, c: (0, 0, 0))],
        out_specs=[
            pl.BlockSpec((tile, width), lambda i, c: (jnp.minimum(i, half - 1), 0)),
            pl.BlockSpec((tile, width), lambda i, c: (jnp.maximum(i - half, 0), 0)),
        ],
    )
    return pl.pallas_call(
        project_back_kernel,
        grid_spec=spec,
        out_shape=[
            jax.ShapeDtypeStruct((rows, width), BF),
            jax.ShapeDtypeStruct((rows, width), F32),
        ],
        cost_estimate=cost(4 * rows * width * wide, 16 * 2**20),
        **params(56),
    )(core, *grads, g1)


def fast_shards(tokens, segment_ids, w_qkv, w_out, w_in, w_back, norm_gains, norm_biases, cotangent):
    both = ("chip", "core", "tensor")
    alike = ("chip", "tensor")
    chip, core, y = [lax.axis_index(n) for n in both]
    chips = lax.axis_size("chip")
    dp_rank = chip * 2 + core
    far = chips // 2
    at_home = core == y

    def ident(q, k, j):
        return (q * 2 + k) * 2 + j

    cells = [(q, k, j) for q in range(chips) for k in range(2) for j in range(2)]
    place_of = {q: p for p, q in enumerate(RING)}
    to_core = [(ident(q, k, j), ident(q, 1 - k, j)) for q, k, j in cells]
    to_y = [(ident(q, k, j), ident(q, k, 1 - j)) for q, k, j in cells]
    diagonal = [(ident(q, k, j), ident(q, j, k)) for q, k, j in cells]
    back = [(ident(q, k, j), ident(q, j, k)) for q, k, j in cells if k != j]
    turn = {d: [(ident(q, k, j), ident(RING[(place_of[q] + d) % chips], k, j)) for q, k, j in cells] for d in (1, -1)}
    hops = [[(ident(q, k, j), ident(q ^ m, k, j)) for q, k, j in cells] for m in (1, 2, 4)]
    near = [0] + [s * d for d in range(1, far) for s in (-1, 1)] + [far]
    table = jnp.array([[RING[(place_of[q] + d) % chips] for d in near] for q in range(chips)], jnp.uint32)
    where = lax.dynamic_index_in_dim(table, chip.astype(jnp.uint32), 0, keepdims=False)

    def chip_at(d):
        return where[near.index(d if d != -far else far)]

    def send(v, pairs):
        return lax.ppermute(v, both, pairs)

    class Gather:
        def __init__(self, unit):
            self.got = {0: unit}
            self.half = unit.shape[0] // 2

        def step(self, n, *deps):
            right, left = after((self.got[1 - n], self.got[n - 1]), *deps)
            if n == far:
                right, left = right[: self.half], left[self.half :]
            self.got[-n], self.got[n] = send(right, turn[1]), send(left, turn[-1])
            return right, left

        def whole(self):
            return assemble(where.astype(jnp.int32), [self.got[d] for d in near[:-1]], self.got[-far], self.got[far])

    class Reduce:
        def __init__(self, blocks):
            self.blocks = blocks
            self.half = blocks.shape[1] // 2
            self.got = None

        def block(self, d):
            return lax.dynamic_index_in_dim(self.blocks, chip_at(d), 0, keepdims=False)

        def step(self, n, *deps):
            half = self.half
            if n == 1:
                whole = self.block(far)
                pieces = after((whole[:half], whole[half:]), *deps)
            else:
                pieces = []
                for way, got in zip((1, -1), after(tuple(self.got), *deps)):
                    mine = self.block(way * (far - n + 1))
                    if n == 2:
                        pad = ((0, half), (0, 0)) if way == 1 else ((half, 0), (0, 0))
                        got = jnp.pad(got, pad)
                    pieces.append((mine.astype(F32) + got.astype(F32)).astype(BF))
            self.got = send(pieces[0], turn[1]), send(pieces[1], turn[-1])
            return tuple(pieces)

        def total(self):
            return self.block(0).astype(F32) + self.got[0].astype(F32) + self.got[1].astype(F32)

    def to_owner(total):
        per = total.shape[0] // 2
        mine = jnp.where(core == 0, total[:per], total[per:])
        theirs = jnp.where(core == 0, total[per:], total[:per]).astype(BF)
        recv = send(theirs, to_core).astype(F32)
        keep = jnp.where(at_home, mine, recv)
        leave = jnp.where(at_home, recv, mine).astype(BF)
        return keep + send(leave, to_y).astype(F32)

    def unit_of(own, across):
        mine = jnp.where(at_home, own, across)
        recv = send(jnp.where(at_home, across, own), to_core)
        return jnp.where(core == 0, jnp.concatenate([mine, recv]), jnp.concatenate([recv, mine]))

    width = tokens.shape[2]
    core_arg = core.astype(jnp.int32)[None]
    heads = w_qkv.shape[2] // HEAD
    slopes = jnp.exp2(-(core * heads + jnp.arange(heads, dtype=jnp.int32) + 1).astype(F32)) * LOG2E

    def reduce_chips(blocks):
        return lax.psum_scatter(blocks.reshape(width, -1), "chip", scatter_dimension=0, tiled=True)

    pad = jnp.zeros((norm_gains.shape[1], 124), F32)
    shard1 = jnp.concatenate(
        [w_qkv[0], w_qkv[1], w_qkv[2], w_out.T, norm_gains.T, norm_biases.T, pad], axis=1
    ).astype(BF)
    low_in = w_in.astype(BF)
    low_back = w_back.T.astype(BF)
    cross1 = send(shard1, to_y)
    seg = jnp.where(at_home, segment_ids, send(segment_ids, to_core))
    seg_col = seg.reshape(-1, 1)
    g1 = Gather(unit_of(shard1, cross1))
    sent = g1.step(1)
    cross_x = send(after(tokens[0], cross1), back)
    sent = g1.step(2)
    cross2 = send(after(low_in, *sent), to_y)
    sent = g1.step(3)
    sent = g1.step(4, cross_x)
    x_own = jnp.where(at_home, tokens[0], after(cross_x, *sent))
    x_oth = send(x_own, to_core)
    g2 = Gather(unit_of(low_in, after(cross2, *sent)))
    sent = g2.step(1, g1.got[-far], g1.got[far])
    cross_y = send(after(cotangent[0], *sent), back)
    wa = g1.whole()
    wide = 4 * heads * HEAD
    gb = wa[:, :, wide : wide + 4].reshape(width, 4).astype(F32).T

    a1, qkv = project(core_arg, after(x_own, *sent), x_oth, gb, wa)
    sent = g2.step(2, qkv)
    mixed0, logs0 = attend(slopes, after(qkv, *sent, cross_y), seg_col, 0, 2)
    sent = g2.step(3, mixed0)
    w2 = lax.all_gather(after(low_back, *sent), both)
    w2 = w2.reshape(2 * chips, 2, *w2.shape[1:])
    mixed1, logs1 = attend(slopes, after(qkv, *sent), seg_col, 2, 2)
    y_own = jnp.where(at_home, cotangent[0], after(cross_y, mixed1))
    y_oth = send(y_own, to_core)
    sent = g2.step(4, mixed1)
    mixed = (after(mixed0, *sent, y_own), mixed1)
    part_recv = send(branch(core_arg, mixed, wa), to_core)
    part_own = branch(core_arg, (after(mixed[0], g2.got[far], g2.got[-far]), mixed[1]), wa, x_own)
    w1 = g2.whole()
    h1, a2_own = residual(after(part_own, w1), part_recv, gb)
    a2_oth = send(a2_own, to_core)
    hidden, slope, gw2 = up(core_arg, a2_own, a2_oth, y_own, y_oth, w1)
    r2 = reduce_chips(gw2)
    f_own, f_oth, d_own, d_oth, gw1 = down(core_arg, a2_own, a2_oth, after(y_own, gw2), y_oth, hidden, slope, w1, w2)
    r1 = reduce_chips(gw1)
    d_recv = send(d_oth, to_core)
    dh1, da_own, sums2 = through_norm(h1, d_own, d_recv, y_own, gb[1:2], True)
    da_oth = send(da_own, to_core)
    f_recv = send(after(f_oth, da_own), to_core)
    do, gwo = head_grad(core_arg, da_own, da_oth, mixed, wa)
    result = (h1 + f_own.astype(F32) + after(f_recv, do).astype(F32)).astype(BF)
    cross_result = send(result, back)
    both_mixed = jnp.concatenate(mixed, axis=1)
    both_logs = jnp.concatenate([logs0, logs1], axis=0)
    grads = attend_back(slopes, after(qkv, do, result), do, both_mixed, both_logs, seg)
    d1_oth, d1_own = project_back(core_arg, after(tuple(grads), r2), wa)
    d1_recv = send(d1_oth, to_core)
    grad_back = to_owner(after(r2, d1_own).astype(F32))
    gwq = project_weight(after(a1, d1_own), gwo, grads)
    result = jnp.where(at_home, result, after(cross_result, gwq))
    rc = Reduce(gwq.reshape(chips, width // chips, -1))
    sent = rc.step(1)
    grad_tokens, sums1 = through_norm(x_own, after(d1_own, *sent, grad_back), d1_recv, dh1, gb[0:1], False)
    cross_tokens = send(grad_tokens, back)
    sent = rc.step(2, sums1)
    sent = rc.step(3, result)
    sent = rc.step(4, cross_tokens)
    grad_in = to_owner(after(r1, *sent).astype(F32))
    sums = jnp.concatenate([sums1[0:1], sums2[0:1], sums1[1:2], sums2[1:2]], axis=0)
    for pairs in (to_core, to_y, *hops):
        sums = sums + send(sums, pairs)
    r3 = to_owner(rc.total())
    grad_tokens = jnp.where(at_home, grad_tokens, cross_tokens)
    per = r3.shape[0]
    wide = 3 * heads * HEAD
    grad_qkv = r3[:, :wide].reshape(per, 3, -1).transpose(1, 0, 2)
    grad_out = r3[:, wide:].T
    sums = lax.dynamic_slice_in_dim(sums, dp_rank.astype(jnp.uint32) * norm_gains.shape[1], norm_gains.shape[1], 1)
    return (result[None], grad_tokens[None], grad_qkv, grad_out, grad_in, grad_back.T, sums[0:2], sums[2:4])


def solution(mesh):
    n_dp, n_tensor = mesh.shape["dp"], mesh.shape["tensor"]
    if n_dp == 16 and n_tensor == 2:
        grid = Mesh(mesh.devices.reshape(n_dp // 2, 2, n_tensor), ("chip", "core", "tensor"))
        body, dp = fast_shards, ("chip", "core")
    else:
        grid, body, dp = mesh, shards, "dp"
    return jax.shard_map(
        body,
        mesh=grid,
        in_specs=(
            P(dp, "tensor", None),
            P(dp, None),
            P(None, dp, "tensor"),
            P("tensor", dp),
            P(dp, "tensor"),
            P("tensor", dp),
            P(None, dp),
            P(None, dp),
            P(dp, "tensor", None),
        ),
        out_specs=(
            P(dp, "tensor", None),
            P(dp, "tensor", None),
            P(None, dp, "tensor"),
            P("tensor", dp),
            P(dp, "tensor"),
            P("tensor", dp),
            P(None, dp),
            P(None, dp),
        ),
        check_vma=False,
    )
```

```python
import math

import jax
import jax.numpy as jnp
from jax import lax
from jax.experimental import pallas as pl
from jax.experimental.pallas import tpu as pltpu
from jax.sharding import Mesh
from jax.sharding import PartitionSpec as P

HEAD = 128
ROW_BLOCK = 512


eps_norm = 1e-05
masked_score = -1e30


def layer_norm(values, gain, shift):
    center = values - jnp.mean(values, axis=-1, keepdims=True)
    spread = jnp.mean(center * center, axis=-1, keepdims=True)
    return center * lax.rsqrt(spread + eps_norm) * gain + shift


def smooth_act(values):
    return jax.nn.gelu(values, approximate=True)


def block_scores(query_rows, keys, seg_rows, seg_all, row_ids, slopes):
    scale = 1.0 / math.sqrt(HEAD)
    raw = jnp.einsum("qhd,khd->hqk", query_rows, keys, preferred_element_type=jnp.float32) * scale
    cols = jnp.arange(keys.shape[0], dtype=jnp.int32)
    dist = (row_ids[:, None] - cols[None, :]).astype(jnp.float32)
    raw = raw - slopes[:, None, None] * dist[None]
    allowed = (cols[None, :] <= row_ids[:, None]) & (seg_rows[:, None] == seg_all[None, :])
    return jnp.where(allowed[None], raw, masked_score)


def attend_forward(qkv_seq, seg_seq, slopes):
    query, keys, values = (qkv_seq[0], qkv_seq[1], qkv_seq[2])
    length = keys.shape[0]

    def one_block(start):
        rows = lax.dynamic_slice_in_dim(query, start, ROW_BLOCK, 0)
        seg_rows = lax.dynamic_slice_in_dim(seg_seq, start, ROW_BLOCK, 0)
        row_ids = start + jnp.arange(ROW_BLOCK, dtype=jnp.int32)
        scores = block_scores(rows, keys, seg_rows, seg_seq, row_ids, slopes)
        top = jnp.max(scores, axis=-1, keepdims=True)
        expo = jnp.exp(scores - top)
        total = jnp.sum(expo, axis=-1, keepdims=True)
        probs = (expo / total).astype(jnp.bfloat16)
        mixed = jnp.einsum("hqk,khd->qhd", probs, values, preferred_element_type=jnp.float32)
        return (mixed, (top + jnp.log(total))[..., 0])

    starts = jnp.arange(length // ROW_BLOCK, dtype=jnp.int32) * ROW_BLOCK
    mixed, log_totals = lax.map(one_block, starts)
    return (mixed.reshape(length, -1), log_totals)


def attend_backward(qkv_seq, seg_seq, log_totals, grad_mixed, slopes):
    query, keys, values = (qkv_seq[0], qkv_seq[1], qkv_seq[2])
    length, heads_here, head_size = keys.shape
    scale = 1.0 / math.sqrt(HEAD)
    grad_rows_all = grad_mixed.reshape(length, heads_here, head_size)

    def one_block(carry, item):
        start, block_totals = item
        rows = lax.dynamic_slice_in_dim(query, start, ROW_BLOCK, 0)
        seg_rows = lax.dynamic_slice_in_dim(seg_seq, start, ROW_BLOCK, 0)
        grad_rows = lax.dynamic_slice_in_dim(grad_rows_all, start, ROW_BLOCK, 0)
        row_ids = start + jnp.arange(ROW_BLOCK, dtype=jnp.int32)
        scores = block_scores(rows, keys, seg_rows, seg_seq, row_ids, slopes)
        probs = jnp.exp(scores - block_totals[..., None])
        grad_probs = jnp.einsum(
            "qhd,khd->hqk", grad_rows, values, preferred_element_type=jnp.float32
        )
        inner = jnp.sum(probs * grad_probs, axis=-1, keepdims=True)
        grad_scores = (probs * (grad_probs - inner)).astype(jnp.bfloat16)
        grad_query = (
            jnp.einsum("hqk,khd->qhd", grad_scores, keys, preferred_element_type=jnp.float32)
            * scale
        )
        grad_keys = (
            carry[0]
            + jnp.einsum("hqk,qhd->khd", grad_scores, rows, preferred_element_type=jnp.float32)
            * scale
        )
        grad_values = carry[1] + jnp.einsum(
            "hqk,qhd->khd",
            probs.astype(jnp.bfloat16),
            grad_rows,
            preferred_element_type=jnp.float32,
        )
        return ((grad_keys, grad_values), grad_query)

    empty = jnp.zeros((length, heads_here, head_size), jnp.float32)
    starts = jnp.arange(length // ROW_BLOCK, dtype=jnp.int32) * ROW_BLOCK
    (grad_keys, grad_values), grad_query = lax.scan(one_block, (empty, empty), (starts, log_totals))
    return jnp.stack([grad_query.reshape(length, heads_here, head_size), grad_keys, grad_values])


def shards(tokens, segment_ids, w_qkv, w_out, w_in, w_back, norm_gains, norm_biases, cotangent):
    low_copies = (
        w_qkv.astype(jnp.bfloat16),
        w_out.astype(jnp.bfloat16),
        w_in.astype(jnp.bfloat16),
        w_back.astype(jnp.bfloat16),
        norm_gains.astype(jnp.bfloat16),
        norm_biases.astype(jnp.bfloat16),
    )
    (
        complete_query_key_value,
        complete_out_weight,
        complete_in_weight,
        complete_back_weight,
        gains_low,
        shifts_low,
    ) = (
        lax.all_gather(low_copies[0], "dp", axis=1, tiled=True),
        lax.all_gather(low_copies[1], "dp", axis=1, tiled=True),
        lax.all_gather(low_copies[2], "dp", axis=0, tiled=True),
        lax.all_gather(low_copies[3], "dp", axis=1, tiled=True),
        lax.all_gather(low_copies[4], "dp", axis=1, tiled=True),
        lax.all_gather(low_copies[5], "dp", axis=1, tiled=True),
    )
    gains = gains_low.astype(jnp.float32)
    shifts = shifts_low.astype(jnp.float32)
    seqs, own_len, width = tokens.shape
    length = segment_ids.shape[1]
    local_width = complete_query_key_value.shape[2]
    heads_here = local_width // HEAD
    rank = lax.axis_index("tensor")
    first_row = rank * own_len
    slopes = jnp.exp2(
        -(rank * heads_here + jnp.arange(heads_here, dtype=jnp.int32) + 1).astype(jnp.float32)
    )
    tokens_f = tokens.astype(jnp.float32)
    tokens_all = lax.all_gather(tokens, "tensor", axis=1, tiled=True).astype(jnp.float32)
    first_normalized = layer_norm(tokens_all, gains[0], shifts[0]).astype(jnp.bfloat16)
    projected = jnp.einsum(
        "gqu,fuk->gfqk",
        first_normalized,
        complete_query_key_value,
        preferred_element_type=jnp.float32,
    ).astype(jnp.bfloat16)
    qkv_heads = projected.reshape(seqs, 3, length, heads_here, HEAD)

    def forward_seq(item):
        return attend_forward(item[0], item[1], slopes)

    mixed, log_totals = lax.map(forward_seq, (qkv_heads, segment_ids))
    attended_values = mixed.astype(jnp.bfloat16)
    attention_slice = jnp.einsum(
        "oin,nh->oih", attended_values, complete_out_weight, preferred_element_type=jnp.float32
    )
    attn_all = lax.psum(attention_slice.astype(jnp.bfloat16), "tensor").astype(jnp.float32)
    resid_all = tokens_all + attn_all
    second_normalized = layer_norm(resid_all, gains[1], shifts[1]).astype(jnp.bfloat16)
    resid = lax.dynamic_slice_in_dim(resid_all, first_row, own_len, 1)
    hidden_preactivation = jnp.einsum(
        "rhi,ip->rhp", second_normalized, complete_in_weight, preferred_element_type=jnp.float32
    )
    hidden_activations = smooth_act(hidden_preactivation).astype(jnp.bfloat16)
    feedforward_slice = jnp.einsum(
        "cow,wv->cov", hidden_activations, complete_back_weight, preferred_element_type=jnp.float32
    )
    ffn_own = lax.psum_scatter(
        feedforward_slice.astype(jnp.bfloat16), "tensor", scatter_dimension=1, tiled=True
    ).astype(jnp.float32)
    result = (resid + ffn_own).astype(jnp.bfloat16)
    cotangent_gathered = lax.all_gather(cotangent, "tensor", axis=1, tiled=True)
    back_weight_gradient_shard = jnp.einsum(
        "ine,inb->eb", hidden_activations, cotangent_gathered, preferred_element_type=jnp.float32
    )
    hidden_gradient = jnp.einsum(
        "jrx,gx->jrg", cotangent_gathered, complete_back_weight, preferred_element_type=jnp.float32
    )
    _, act_pull = jax.vjp(smooth_act, hidden_preactivation)
    preactivation_gradient = act_pull(hidden_gradient)[0].astype(jnp.bfloat16)
    in_weight_gradient_shard = jnp.einsum(
        "bkw,bkz->wz", second_normalized, preactivation_gradient, preferred_element_type=jnp.float32
    )
    second_norm_slice = jnp.einsum(
        "kyj,tj->kyt",
        preactivation_gradient,
        complete_in_weight,
        preferred_element_type=jnp.float32,
    )
    grad_norm2 = lax.psum_scatter(
        second_norm_slice.astype(jnp.bfloat16), "tensor", scatter_dimension=1, tiled=True
    ).astype(jnp.float32)
    _, second_pull = jax.vjp(layer_norm, resid, gains[1], shifts[1])
    grad_resid_norm, grad_gain2, grad_shift2 = second_pull(grad_norm2)
    grad_resid = cotangent.astype(jnp.float32) + grad_resid_norm
    attention_gradient_gathered = lax.all_gather(
        grad_resid.astype(jnp.bfloat16), "tensor", axis=1, tiled=True
    )
    grad_out_local = jnp.einsum(
        "xwq,xwr->qr",
        attended_values,
        attention_gradient_gathered,
        preferred_element_type=jnp.float32,
    )
    grad_attended = jnp.einsum(
        "wik,jk->wij",
        attention_gradient_gathered,
        complete_out_weight,
        preferred_element_type=jnp.float32,
    ).astype(jnp.bfloat16)

    def backward_seq(item):
        return attend_backward(item[0], item[1], item[2], item[3], slopes)

    grad_heads = lax.map(backward_seq, (qkv_heads, segment_ids, log_totals, grad_attended))
    projection_gradient = grad_heads.reshape(seqs, 3, length, local_width).astype(jnp.bfloat16)
    grad_qkv_local = jnp.einsum(
        "phb,pthw->tbw", first_normalized, projection_gradient, preferred_element_type=jnp.float32
    )
    norm1_part = jnp.einsum(
        "zjyw,juw->zyu",
        projection_gradient,
        complete_query_key_value,
        preferred_element_type=jnp.float32,
    )
    grad_norm1 = lax.psum_scatter(
        norm1_part.astype(jnp.bfloat16), "tensor", scatter_dimension=1, tiled=True
    ).astype(jnp.float32)
    _, first_pull = jax.vjp(layer_norm, tokens_f, gains[0], shifts[0])
    grad_tok_norm, grad_gain1, grad_shift1 = first_pull(grad_norm1)
    grad_tokens = (grad_resid + grad_tok_norm).astype(jnp.bfloat16)
    gain_terms = jnp.stack([grad_gain1, grad_gain2])
    shift_terms = jnp.stack([grad_shift1, grad_shift2])
    gain_sum, shift_sum = lax.psum((gain_terms, shift_terms), "tensor")
    summed = (
        lax.psum_scatter(
            grad_qkv_local.astype(jnp.bfloat16), "dp", scatter_dimension=1, tiled=True
        ).astype(jnp.float32),
        lax.psum_scatter(
            grad_out_local.astype(jnp.bfloat16), "dp", scatter_dimension=1, tiled=True
        ).astype(jnp.float32),
        lax.psum_scatter(
            in_weight_gradient_shard.astype(jnp.bfloat16), "dp", scatter_dimension=0, tiled=True
        ).astype(jnp.float32),
        lax.psum_scatter(
            back_weight_gradient_shard.astype(jnp.bfloat16), "dp", scatter_dimension=1, tiled=True
        ).astype(jnp.float32),
        lax.psum_scatter(
            gain_sum.astype(jnp.bfloat16), "dp", scatter_dimension=1, tiled=True
        ).astype(jnp.float32),
        lax.psum_scatter(
            shift_sum.astype(jnp.bfloat16), "dp", scatter_dimension=1, tiled=True
        ).astype(jnp.float32),
    )
    return (result, grad_tokens, summed[0], summed[1], summed[2], summed[3], summed[4], summed[5])


LOG2E = math.log2(math.e)
SCALE2 = LOG2E / math.sqrt(HEAD)
BLK = 512
BF = jnp.bfloat16
F32 = jnp.float32
NN = (((1,), (0,)), ((), ()))
NT = (((1,), (1,)), ((), ()))
TN = (((0,), (0,)), ((), ()))
RING = (0, 2, 4, 6, 7, 5, 3, 1)


def mm(a, b, dims):
    return lax.dot_general(a, b, dims, preferred_element_type=F32)


def params(mib, cost=None):
    return dict(compiler_params=pltpu.CompilerParams(vmem_limit_bytes=mib * 2**20))


def after(v, *deps):
    return lax.optimization_barrier((v,) + deps)[0]


def cost(flops, nbytes, trans=0):
    return pl.CostEstimate(flops=1024, bytes_accessed=1024, transcendentals=0)


def normalize(v):
    c = v - jnp.mean(v, axis=-1, keepdims=True)
    r = lax.rsqrt(jnp.mean(c * c, axis=-1, keepdims=True) + eps_norm)
    return c * r, r


def norm_back(v, dout, gain):
    cn, r = normalize(v)
    t = dout * gain
    dv = r * (t - jnp.mean(t, axis=-1, keepdims=True) - cn * jnp.mean(t * cn, axis=-1, keepdims=True))
    return dv, jnp.sum(dout * cn, axis=0, keepdims=True), jnp.sum(dout, axis=0, keepdims=True)


def project_kernel(core, xa, xb, gb, w, a1_out, qkv_out):
    step = pl.program_id(0)
    half = pl.num_programs(0) // 2
    x = jnp.where(step < half, xa[...], xb[...]).astype(F32)
    a1 = (normalize(x)[0] * gb[0:1] + gb[2:3]).astype(BF)
    a1_out[...] = a1
    weight = w[...].reshape(w.shape[0] * w.shape[1], w.shape[2])
    qkv_out[...] = mm(a1, weight, NN).astype(BF)


def project(core, x_own, x_oth, gb, g1):
    rows, width = x_own.shape
    tile = 512
    half = rows // tile
    chips, per, _ = g1.shape
    wide = 3 * 512
    spec = pltpu.PrefetchScalarGridSpec(
        num_scalar_prefetch=1,
        grid=(2 * half,),
        in_specs=[
            pl.BlockSpec((tile, width), lambda i, c: (jnp.minimum(i, half - 1), 0)),
            pl.BlockSpec((tile, width), lambda i, c: (jnp.maximum(i - half, 0), 0)),
            pl.BlockSpec((4, width), lambda i, c: (0, 0)),
            pl.BlockSpec((chips, per, wide), lambda i, c: (0, 0, 0)),
        ],
        out_specs=[
            pl.BlockSpec((tile, width), lambda i, c: (i % half + half * ((i // half) ^ c[0]), 0)),
            pl.BlockSpec((tile, wide), lambda i, c: (i % half + half * ((i // half) ^ c[0]), 0)),
        ],
    )
    return pl.pallas_call(
        project_kernel,
        grid_spec=spec,
        out_shape=[
            jax.ShapeDtypeStruct((2 * rows, width), BF),
            jax.ShapeDtypeStruct((2 * rows, wide), BF),
        ],
        cost_estimate=cost(4 * rows * width * wide, 12 * 2**20),
        **params(48),
    )(core, x_own, x_oth, gb, g1)


def attend_kernel(slopes, q_ref, k_ref, v_ref, seg_ref, o_ref, l_ref, s_ref):
    m2 = slopes[pl.program_id(0)]
    blocks = q_ref.shape[0] // BLK
    lane = lax.broadcasted_iota(jnp.int32, (1, BLK), 1)
    row = lax.broadcasted_iota(jnp.int32, (BLK, 1), 0)
    for i in range(blocks):
        q = q_ref[i * BLK : (i + 1) * BLK, :]
        seg = seg_ref[i * BLK : (i + 1) * BLK, :]
        top = jnp.full((BLK, 128), masked_score, F32)
        for j in range(i + 1):
            cols = slice(j * BLK, (j + 1) * BLK)
            bias = m2 * (lane + (j - i) * BLK).astype(F32)
            s = mm(q, k_ref[cols, :], NT) * SCALE2 + bias
            allowed = (lane + j * BLK) >= seg
            if j == i:
                allowed = allowed & (lane <= row)
            s = jnp.where(allowed, s, masked_score)
            s_ref[:, cols] = s
            for c in range(0, BLK, 128):
                top = jnp.maximum(top, s[:, c : c + 128])
        top = jnp.max(top, axis=1, keepdims=True)
        total = jnp.zeros((BLK, 128), F32)
        mixed = jnp.zeros((BLK, HEAD), F32)
        for j in range(i + 1):
            cols = slice(j * BLK, (j + 1) * BLK)
            p = jnp.exp2(s_ref[:, cols] - top)
            for c in range(0, BLK, 128):
                total = total + p[:, c : c + 128]
            mixed = mixed + mm(p.astype(BF), v_ref[cols, :], NN)
        total = jnp.sum(total, axis=1, keepdims=True)
        o_ref[i * BLK : (i + 1) * BLK, :] = (mixed / total).astype(BF)
        logs = jnp.broadcast_to(top + jnp.log2(total), (BLK, 128))
        l_ref[0, :, i * BLK : (i + 1) * BLK] = logs.T[0:1, :]


def attend(slopes, qkv, seg_col, first, count):
    length = qkv.shape[0]
    heads = qkv.shape[1] // (3 * HEAD)
    spec = pltpu.PrefetchScalarGridSpec(
        num_scalar_prefetch=1,
        grid=(count,),
        in_specs=[
            pl.BlockSpec((length, HEAD), lambda h, s: (0, first + h)),
            pl.BlockSpec((length, HEAD), lambda h, s: (0, heads + first + h)),
            pl.BlockSpec((length, HEAD), lambda h, s: (0, 2 * heads + first + h)),
            pl.BlockSpec((length, 1), lambda h, s: (0, 0)),
        ],
        out_specs=[
            pl.BlockSpec((length, HEAD), lambda h, s: (0, h)),
            pl.BlockSpec((1, 1, length), lambda h, s: (h, 0, 0)),
        ],
        scratch_shapes=[pltpu.VMEM((BLK, length), F32)],
    )
    return pl.pallas_call(
        attend_kernel,
        grid_spec=spec,
        out_shape=[
            jax.ShapeDtypeStruct((length, count * HEAD), BF),
            jax.ShapeDtypeStruct((count, 1, length), F32),
        ],
        cost_estimate=cost(count * 4 * length * length * HEAD, 3 * count * 2**20, count * length * length),
        **params(48),
    )(lax.slice_in_dim(slopes, first, first + count), qkv, qkv, qkv, seg_col)


def attend_back_kernel(slopes, q_ref, k_ref, v_ref, do_ref, o_ref, l_ref, seg_ref, dq_ref, dk_ref, dv_ref, acc, inner):
    m2 = slopes[pl.program_id(0)]
    blocks = q_ref.shape[0] // BLK
    lane = lax.broadcasted_iota(jnp.int32, (1, BLK), 1)
    row = lax.broadcasted_iota(jnp.int32, (BLK, 1), 0)
    for i in range(blocks):
        rows = slice(i * BLK, (i + 1) * BLK)
        d = jnp.sum(do_ref[rows, :].astype(F32) * o_ref[rows, :].astype(F32), axis=1, keepdims=True)
        inner[:, rows] = jnp.broadcast_to(d, (BLK, 128)).T[0:8, :]
    for j in range(blocks):
        cols = slice(j * BLK, (j + 1) * BLK)
        kj, vj = k_ref[cols, :], v_ref[cols, :]
        dk = jnp.zeros((BLK, HEAD), F32)
        dv = jnp.zeros((BLK, HEAD), F32)
        for i in range(j, blocks):
            rows = slice(i * BLK, (i + 1) * BLK)
            qi, doi = q_ref[rows, :], do_ref[rows, :]
            bias = m2 * (row + (j - i) * BLK).astype(F32)
            s = mm(kj, qi, NT) * SCALE2 + bias - l_ref[0, :, rows]
            allowed = (row + j * BLK) >= seg_ref[:, rows]
            if j == i:
                allowed = allowed & (row <= lane)
            p = jnp.exp2(jnp.where(allowed, s, masked_score))
            ds = (p * (mm(vj, doi, NT) - inner[0:1, rows])).astype(BF)
            dv = dv + mm(p.astype(BF), doi, NN)
            dk = dk + mm(ds, qi, NN)
            dq = mm(ds, kj, TN)
            if j == 0:
                acc[rows, :] = dq
            else:
                acc[rows, :] += dq
        dk_ref[cols, :] = (dk * (1.0 / math.sqrt(HEAD))).astype(BF)
        dv_ref[cols, :] = dv.astype(BF)
    dq_ref[...] = (acc[...] * (1.0 / math.sqrt(HEAD))).astype(BF)


def attend_back(slopes, qkv, grad, mixed, logs, seg_row):
    length = qkv.shape[0]
    heads = qkv.shape[1] // (3 * HEAD)

    def column(at):
        return pl.BlockSpec((length, HEAD), lambda h, s: (0, at + h))

    spec = pltpu.PrefetchScalarGridSpec(
        num_scalar_prefetch=1,
        grid=(heads,),
        in_specs=[
            column(0),
            column(heads),
            column(2 * heads),
            column(0),
            column(0),
            pl.BlockSpec((1, 1, length), lambda h, s: (h, 0, 0)),
            pl.BlockSpec((1, length), lambda h, s: (0, 0)),
        ],
        out_specs=[column(0)] * 3,
        scratch_shapes=[pltpu.VMEM((length, HEAD), F32), pltpu.VMEM((8, length), F32)],
    )
    return pl.pallas_call(
        attend_back_kernel,
        grid_spec=spec,
        out_shape=[jax.ShapeDtypeStruct((length, heads * HEAD), BF)] * 3,
        cost_estimate=cost(heads * 10 * length * length * HEAD, 5 * heads * 2**20, heads * length * length),
        **params(48),
    )(slopes, qkv, qkv, qkv, grad, mixed, logs, seg_row)


def branch_oth_kernel(core, oa, ob, w, out):
    weight = w[...].reshape(w.shape[0] * w.shape[1], w.shape[2])
    out[...] = mm(jnp.concatenate([oa[...], ob[...]], axis=1), weight, NT).astype(BF)


def branch_own_kernel(core, oa, ob, w, x_ref, out):
    weight = w[...].reshape(w.shape[0] * w.shape[1], w.shape[2])
    out[...] = x_ref[...].astype(F32) + mm(jnp.concatenate([oa[...], ob[...]], axis=1), weight, NT)


def branch(core, mixed, weights, x_own=None):
    rows = mixed[0].shape[0] // 2
    chips, per, _ = weights.shape
    width = chips * per
    tile = 512
    half = rows // tile
    own = x_own is not None
    own_rows = pl.BlockSpec((tile, width), lambda i, c: (i, 0))

    def place(i, c):
        return (i + half * (c[0] if own else 1 - c[0]), 0)

    spec = pltpu.PrefetchScalarGridSpec(
        num_scalar_prefetch=1,
        grid=(half,),
        in_specs=[pl.BlockSpec((tile, 256), place)] * 2
        + [pl.BlockSpec((chips, per, 512), lambda i, c: (0, 0, 3))]
        + ([own_rows] if own else []),
        out_specs=own_rows,
    )
    return pl.pallas_call(
        branch_own_kernel if own else branch_oth_kernel,
        grid_spec=spec,
        out_shape=jax.ShapeDtypeStruct((rows, width), F32 if own else BF),
        cost_estimate=cost(2 * rows * width * 512, 6 * 2**20),
        **params(48),
    )(core, *mixed, weights, *([x_own] if own else []))


def residual_kernel(part, recv, gb, h_out, a2_out):
    h = part[...] + recv[...].astype(F32)
    h_out[...] = h
    a2_out[...] = (normalize(h)[0] * gb[1:2] + gb[3:4]).astype(BF)


def residual(part, recv, gb):
    rows, width = part.shape
    tile = 256
    spec = pl.BlockSpec((tile, width), lambda i: (i, 0))
    return pl.pallas_call(
        residual_kernel,
        grid=(rows // tile,),
        in_specs=[spec, spec, pl.BlockSpec((4, width), lambda i: (0, 0))],
        out_specs=[spec, spec],
        out_shape=[
            jax.ShapeDtypeStruct((rows, width), F32),
            jax.ShapeDtypeStruct((rows, width), BF),
        ],
        cost_estimate=cost(20 * rows * width, 12 * 2**20),
        **params(32),
    )(part, recv, gb)


def up_kernel(core, aa, ab, ya, yb, w_ref, g_out, s_out, gw_out, acc):
    step = pl.program_id(0)
    steps = pl.num_programs(0)
    a2 = jnp.where(step < steps // 2, aa[...], ab[...])
    dyt = jnp.where(step < steps // 2, ya[...], yb[...]).T
    chips, per, hidden = w_ref.shape
    chunk = 512
    c0, c1 = math.sqrt(2.0 / math.pi), 0.044715

    @pl.when(step == 0)
    def _():
        acc[...] = jnp.zeros_like(acc)

    def product(c):
        return mm(a2, w_ref[:, :, c : c + chunk].reshape(chips * per, chunk), NN)

    u, held = product(0), []
    for c in range(0, hidden, chunk):
        cols = slice(c, c + chunk)
        later = product(c + chunk) if c + chunk < hidden else None
        sq = u * u
        th = jnp.tanh(u * (c0 + c0 * c1 * sq))
        hp = 0.5 + 0.5 * th
        g = (u * hp).astype(BF)
        g_out[:, cols] = g
        s_out[:, cols] = (hp + (0.5 * u) * (1.0 - th * th) * (c0 + 3.0 * c0 * c1 * sq)).astype(BF)
        held.append((cols, g))
        if c > 0:
            acc[:, held[-2][0]] += mm(dyt, held[-2][1], NN)
        u = later
    acc[:, held[-1][0]] += mm(dyt, held[-1][1], NN)

    @pl.when(step == steps - 1)
    def _():
        gw_out[...] = acc[...].astype(BF).reshape(gw_out.shape)


def halves(tile, width, half):
    return [
        pl.BlockSpec((tile, width), lambda i, *c: (jnp.minimum(i, half - 1), 0)),
        pl.BlockSpec((tile, width), lambda i, *c: (jnp.maximum(i - half, 0), 0)),
    ]


def ringed(w):
    return pl.BlockSpec(w.shape, lambda i, *c: (0, 0, 0), pipeline_mode=pl.Buffered(1))


def gathered(w):
    return pl.BlockSpec((w.shape[0], 1) + w.shape[2:], lambda i, c: (0, c[0], 0, 0), pipeline_mode=pl.Buffered(1))


def up(core, a_own, a_oth, y_own, y_oth, w1):
    rows, width = a_own.shape
    chips, _, hidden = w1.shape
    tile = 512
    out = pl.BlockSpec((tile, hidden), lambda i, c: (i, 0))
    spec = pltpu.PrefetchScalarGridSpec(
        num_scalar_prefetch=1,
        grid=(2 * rows // tile,),
        in_specs=halves(tile, width, rows // tile) * 2 + [ringed(w1)],
        out_specs=[
            out,
            out,
            pl.BlockSpec((chips, width // chips, hidden), lambda i, c: (0, 0, 0), pipeline_mode=pl.Buffered(1)),
        ],
        scratch_shapes=[pltpu.VMEM((width, hidden), F32)],
    )
    return pl.pallas_call(
        up_kernel,
        grid_spec=spec,
        out_shape=[jax.ShapeDtypeStruct((2 * rows, hidden), BF)] * 2
        + [jax.ShapeDtypeStruct((chips, width // chips, hidden), BF)],
        cost_estimate=cost(8 * rows * width * hidden, 32 * 2**20, 2 * rows * hidden),
        **params(60),
    )(core, a_own, a_oth, y_own, y_oth, w1)


def down_kernel(core, aa, ab, ya, yb, g_ref, s_ref, w1_ref, w2_ref, f_own, f_oth, d_own, d_oth, gw_out, a2t_s, du_s):
    step = pl.program_id(0)
    steps = pl.num_programs(0)
    half = steps // 2
    chips, per, hidden = w1_ref.shape
    width = chips * per
    tile = aa.shape[0]
    rows = pl.ds(pl.multiple_of(step * tile, tile), tile)
    a2t_s[:, rows] = jnp.where(step < half, aa[...], ab[...]).T
    dy = jnp.where(step < half, ya[...], yb[...])
    chunk = 512
    for c in range(0, hidden, chunk):
        cols = slice(c, c + chunk)
        dg = mm(dy, w2_ref[:, 0, :, cols].reshape(width, chunk), NN)
        du_s[rows, cols] = (dg * s_ref[:, cols].astype(F32)).astype(BF)
    f = mm(g_ref[...], w2_ref[:, 0].reshape(width, hidden), NT).astype(BF)
    d = mm(du_s[rows, :], w1_ref[...].reshape(width, hidden), NT).astype(BF)

    @pl.when(step < half)
    def _():
        f_own[...] = f
        d_own[...] = d

    @pl.when(step >= half)
    def _():
        f_oth[...] = f
        d_oth[...] = d

    @pl.when(step == steps - 1)
    def _():
        for c in range(0, hidden, chunk):
            cols = slice(c, c + chunk)
            gw_out[:, :, cols] = mm(a2t_s[...], du_s[:, cols], NN).astype(BF).reshape(chips, per, chunk)


def down(core, a_own, a_oth, y_own, y_oth, hidden_units, slope, w1, w2):
    rows, width = a_own.shape
    chips, per, hidden = w1.shape
    tile = 512
    units = pl.BlockSpec((tile, hidden), lambda i, c: (i, 0))
    spec = pltpu.PrefetchScalarGridSpec(
        num_scalar_prefetch=1,
        grid=(2 * rows // tile,),
        in_specs=halves(tile, width, rows // tile) * 2 + [units, units, ringed(w1), gathered(w2)],
        out_specs=halves(tile, width, rows // tile) * 2
        + [pl.BlockSpec((chips, per, hidden), lambda i, c: (0, 0, 0), pipeline_mode=pl.Buffered(1))],
        scratch_shapes=[pltpu.VMEM((width, 2 * rows), BF), pltpu.VMEM((2 * rows, hidden), BF)],
    )
    return pl.pallas_call(
        down_kernel,
        grid_spec=spec,
        out_shape=[jax.ShapeDtypeStruct((rows, width), BF)] * 4
        + [jax.ShapeDtypeStruct((chips, per, hidden), BF)],
        cost_estimate=cost(16 * rows * width * hidden, 40 * 2**20),
        **params(60),
    )(core, a_own, a_oth, y_own, y_oth, hidden_units, slope, w1, w2)


def assemble_kernel(order, *refs):
    *pieces, far_a, far_b, out, sems = refs
    half = far_a.shape[0]
    n = len(pieces)
    copies = [pltpu.make_async_copy(p, out.at[order[i]], sems.at[i]) for i, p in enumerate(pieces)]
    copies.append(pltpu.make_async_copy(far_a, out.at[order[n], pl.ds(0, half)], sems.at[n]))
    copies.append(pltpu.make_async_copy(far_b, out.at[order[n], pl.ds(half, half)], sems.at[n + 1]))
    for c in copies:
        c.start()
    for c in copies:
        c.wait()


def assemble(order, pieces, far_a, far_b):
    unit = pieces[0]
    any_ = pl.BlockSpec(memory_space=pl.ANY)
    spec = pltpu.PrefetchScalarGridSpec(
        num_scalar_prefetch=1,
        grid=(1,),
        in_specs=[pl.BlockSpec(p.shape, lambda i, o: (0, 0)) for p in (*pieces, far_a, far_b)],
        out_specs=any_,
        scratch_shapes=[pltpu.SemaphoreType.DMA((len(pieces) + 2,))],
    )
    return pl.pallas_call(
        assemble_kernel,
        grid_spec=spec,
        out_shape=jax.ShapeDtypeStruct((len(pieces) + 1,) + unit.shape, unit.dtype),
        cost_estimate=cost(0, 4 * (len(pieces) + 1) * unit.size),
    )(order, *pieces, far_a, far_b)


def norm_back_kernel(v_ref, part, recv, skip, gain, dv_out, low_out, sums):
    @pl.when(pl.program_id(0) == 0)
    def _():
        sums[...] = jnp.zeros_like(sums)

    dout = part[...].astype(F32) + recv[...].astype(F32)
    dv, dg, db = norm_back(v_ref[...].astype(F32), dout, gain[...])
    dv = skip[...].astype(F32) + dv
    if dv_out is not None:
        dv_out[...] = dv
    low_out[...] = dv.astype(BF)
    sums[0:1] += dg
    sums[1:2] += db


def through_norm(v, part, recv, skip, gain, keep):
    rows, width = v.shape
    tile = 256
    spec = pl.BlockSpec((tile, width), lambda i: (i, 0))
    kernel = norm_back_kernel if keep else (lambda *r: norm_back_kernel(*r[:5], None, *r[5:]))
    outs = [jax.ShapeDtypeStruct((rows, width), F32)] if keep else []
    return pl.pallas_call(
        kernel,
        grid=(rows // tile,),
        in_specs=[spec] * 4 + [pl.BlockSpec((1, width), lambda i: (0, 0))],
        out_specs=[spec] * (1 + keep) + [pl.BlockSpec((2, width), lambda i: (0, 0))],
        out_shape=outs + [jax.ShapeDtypeStruct((rows, width), BF), jax.ShapeDtypeStruct((2, width), F32)],
        cost_estimate=cost(30 * rows * width, 16 * 2**20),
        **params(32),
    )(v, part, recv, skip, gain)


def head_grad_kernel(core, da, db, oa, ob, w, do_out, gw_out, acc):
    step = pl.program_id(0)
    steps = pl.num_programs(0)
    d = jnp.where(step < steps // 2, da[...], db[...])
    weight = w[...].reshape(w.shape[0] * w.shape[1], w.shape[2])
    do_out[...] = mm(d, weight, NN).astype(BF)

    @pl.when(step == 0)
    def _():
        acc[...] = jnp.zeros_like(acc)

    acc[...] += mm(d, jnp.concatenate([oa[...], ob[...]], axis=1), TN)

    @pl.when(step == steps - 1)
    def _():
        gw_out[...] = acc[...].astype(BF)


def head_grad(core, d_own, d_oth, mixed, g1):
    rows, width = d_own.shape
    tile = 512
    half = rows // tile
    chips, per, _ = g1.shape
    spec = pltpu.PrefetchScalarGridSpec(
        num_scalar_prefetch=1,
        grid=(2 * half,),
        in_specs=[
            pl.BlockSpec((tile, width), lambda i, c: (jnp.minimum(i, half - 1), 0)),
            pl.BlockSpec((tile, width), lambda i, c: (jnp.maximum(i - half, 0), 0)),
            pl.BlockSpec((tile, 256), lambda i, c: (i % half + half * ((i // half) ^ c[0]), 0)),
            pl.BlockSpec((tile, 256), lambda i, c: (i % half + half * ((i // half) ^ c[0]), 0)),
            pl.BlockSpec((chips, per, 512), lambda i, c: (0, 0, 3)),
        ],
        out_specs=[
            pl.BlockSpec((tile, 512), lambda i, c: (i % half + half * ((i // half) ^ c[0]), 0)),
            pl.BlockSpec((width, 512), lambda i, c: (0, 0)),
        ],
        scratch_shapes=[pltpu.VMEM((width, 512), F32)],
    )
    return pl.pallas_call(
        head_grad_kernel,
        grid_spec=spec,
        out_shape=[
            jax.ShapeDtypeStruct((2 * rows, 512), BF),
            jax.ShapeDtypeStruct((width, 512), BF),
        ],
        cost_estimate=cost(8 * rows * width * 512, 12 * 2**20),
        **params(48),
    )(core, d_own, d_oth, *mixed, g1)


def project_weight_kernel(a1, gwo, *refs):
    *grads, gw_out, acc = refs
    step = pl.program_id(0)
    grad = jnp.concatenate([g[...] for g in grads], axis=1)
    wide = grad.shape[1]

    @pl.when(step == 0)
    def _():
        acc[...] = jnp.zeros_like(acc)
        gw_out[:, wide:] = gwo[...]

    acc[...] += mm(a1[...], grad, TN)

    @pl.when(step == pl.num_programs(0) - 1)
    def _():
        gw_out[:, :wide] = acc[...].astype(BF)


def project_weight(a1, gwo, grads):
    rows2, width = a1.shape
    tile = 512
    wide = sum(g.shape[1] for g in grads)
    total = wide + gwo.shape[1]
    return pl.pallas_call(
        project_weight_kernel,
        grid=(rows2 // tile,),
        in_specs=[pl.BlockSpec((tile, width), lambda i: (i, 0)), pl.BlockSpec(gwo.shape, lambda i: (0, 0))]
        + [pl.BlockSpec((tile, g.shape[1]), lambda i: (i, 0)) for g in grads],
        out_specs=pl.BlockSpec((width, total), lambda i: (0, 0)),
        scratch_shapes=[pltpu.VMEM((width, wide), F32)],
        out_shape=jax.ShapeDtypeStruct((width, total), BF),
        cost_estimate=cost(2 * rows2 * width * wide, 14 * 2**20),
        **params(56),
    )(a1, gwo, *grads)


def project_back_kernel(core, *refs):
    *grads, w, d_oth, d_own = refs
    step = pl.program_id(0)
    steps = pl.num_programs(0)
    grad = jnp.concatenate([g[...] for g in grads], axis=1)
    weight = w[...].reshape(w.shape[0] * w.shape[1], w.shape[2])
    part = mm(grad, weight, NT)

    @pl.when(step < steps // 2)
    def _():
        d_oth[...] = part.astype(BF)

    @pl.when(step >= steps // 2)
    def _():
        d_own[...] = part


def project_back(core, grads, g1):
    rows = grads[0].shape[0] // 2
    chips, per, _ = g1.shape
    width = chips * per
    tile = 512
    half = rows // tile
    wide = sum(g.shape[1] for g in grads)

    def place(i, c):
        return (i % half + half * (1 - (i // half) ^ c[0]), 0)

    spec = pltpu.PrefetchScalarGridSpec(
        num_scalar_prefetch=1,
        grid=(2 * half,),
        in_specs=[pl.BlockSpec((tile, g.shape[1]), place) for g in grads]
        + [pl.BlockSpec((chips, per, wide), lambda i, c: (0, 0, 0))],
        out_specs=[
            pl.BlockSpec((tile, width), lambda i, c: (jnp.minimum(i, half - 1), 0)),
            pl.BlockSpec((tile, width), lambda i, c: (jnp.maximum(i - half, 0), 0)),
        ],
    )
    return pl.pallas_call(
        project_back_kernel,
        grid_spec=spec,
        out_shape=[
            jax.ShapeDtypeStruct((rows, width), BF),
            jax.ShapeDtypeStruct((rows, width), F32),
        ],
        cost_estimate=cost(4 * rows * width * wide, 16 * 2**20),
        **params(56),
    )(core, *grads, g1)


def fast_shards(tokens, segment_ids, w_qkv, w_out, w_in, w_back, norm_gains, norm_biases, cotangent):
    both = ("chip", "core", "tensor")
    alike = ("chip", "tensor")
    chip, core, y = [lax.axis_index(n) for n in both]
    chips = lax.axis_size("chip")
    dp_rank = chip * 2 + core
    far = chips // 2
    at_home = core == y

    def ident(q, k, j):
        return (q * 2 + k) * 2 + j

    cells = [(q, k, j) for q in range(chips) for k in range(2) for j in range(2)]
    place_of = {q: p for p, q in enumerate(RING)}
    to_core = [(ident(q, k, j), ident(q, 1 - k, j)) for q, k, j in cells]
    to_y = [(ident(q, k, j), ident(q, k, 1 - j)) for q, k, j in cells]
    diagonal = [(ident(q, k, j), ident(q, j, k)) for q, k, j in cells]
    back = [(ident(q, k, j), ident(q, j, k)) for q, k, j in cells if k != j]
    turn = {d: [(ident(q, k, j), ident(RING[(place_of[q] + d) % chips], k, j)) for q, k, j in cells] for d in (1, -1)}
    hops = [[(ident(q, k, j), ident(q ^ m, k, j)) for q, k, j in cells] for m in (1, 2, 4)]
    near = [0] + [s * d for d in range(1, far) for s in (-1, 1)] + [far]
    table = jnp.array([[RING[(place_of[q] + d) % chips] for d in near] for q in range(chips)], jnp.uint32)
    where = lax.dynamic_index_in_dim(table, chip.astype(jnp.uint32), 0, keepdims=False)

    def chip_at(d):
        return where[near.index(d if d != -far else far)]

    def send(v, pairs):
        return lax.ppermute(v, both, pairs)

    class Gather:
        def __init__(self, unit):
            self.got = {0: unit}
            self.half = unit.shape[0] // 2

        def step(self, n, *deps):
            right, left = after((self.got[1 - n], self.got[n - 1]), *deps)
            if n == far:
                right, left = right[: self.half], left[self.half :]
            self.got[-n], self.got[n] = send(right, turn[1]), send(left, turn[-1])
            return right, left

        def whole(self):
            return assemble(where.astype(jnp.int32), [self.got[d] for d in near[:-1]], self.got[-far], self.got[far])

    class Reduce:
        def __init__(self, blocks):
            self.blocks = blocks
            self.half = blocks.shape[1] // 2
            self.got = None

        def block(self, d):
            return lax.dynamic_index_in_dim(self.blocks, chip_at(d), 0, keepdims=False)

        def step(self, n, *deps):
            half = self.half
            if n == 1:
                whole = self.block(far)
                pieces = after((whole[:half], whole[half:]), *deps)
            else:
                pieces = []
                for way, got in zip((1, -1), after(tuple(self.got), *deps)):
                    mine = self.block(way * (far - n + 1))
                    if n == 2:
                        pad = ((0, half), (0, 0)) if way == 1 else ((half, 0), (0, 0))
                        got = jnp.pad(got, pad)
                    pieces.append((mine.astype(F32) + got.astype(F32)).astype(BF))
            self.got = send(pieces[0], turn[1]), send(pieces[1], turn[-1])
            return tuple(pieces)

        def total(self):
            return self.block(0).astype(F32) + self.got[0].astype(F32) + self.got[1].astype(F32)

    def to_owner(total):
        per = total.shape[0] // 2
        mine = jnp.where(core == 0, total[:per], total[per:])
        theirs = jnp.where(core == 0, total[per:], total[:per]).astype(BF)
        recv = send(theirs, to_core).astype(F32)
        keep = jnp.where(at_home, mine, recv)
        leave = jnp.where(at_home, recv, mine).astype(BF)
        return keep + send(leave, to_y).astype(F32)

    def unit_of(own, across):
        mine = jnp.where(at_home, own, across)
        recv = send(jnp.where(at_home, across, own), to_core)
        return jnp.where(core == 0, jnp.concatenate([mine, recv]), jnp.concatenate([recv, mine]))

    width = tokens.shape[2]
    core_arg = core.astype(jnp.int32)[None]
    heads = w_qkv.shape[2] // HEAD
    slopes = jnp.exp2(-(core * heads + jnp.arange(heads, dtype=jnp.int32) + 1).astype(F32)) * LOG2E

    def reduce_chips(blocks):
        return lax.psum_scatter(blocks.reshape(width, -1), "chip", scatter_dimension=0, tiled=True)

    pad = jnp.zeros((norm_gains.shape[1], 124), F32)
    shard1 = jnp.concatenate(
        [w_qkv[0], w_qkv[1], w_qkv[2], w_out.T, norm_gains.T, norm_biases.T, pad], axis=1
    ).astype(BF)
    low_in = w_in.astype(BF)
    low_back = w_back.T.astype(BF)
    cross1 = send(shard1, to_y)
    seg = jnp.where(at_home, segment_ids, send(segment_ids, to_core))
    seg_col = seg.reshape(-1, 1)
    g1 = Gather(unit_of(shard1, cross1))
    sent = g1.step(1)
    cross_x = send(after(tokens[0], cross1), back)
    sent = g1.step(2)
    cross2 = send(after(low_in, *sent), to_y)
    sent = g1.step(3)
    sent = g1.step(4, cross_x)
    x_own = jnp.where(at_home, tokens[0], after(cross_x, *sent))
    x_oth = send(x_own, to_core)
    g2 = Gather(unit_of(low_in, after(cross2, *sent)))
    sent = g2.step(1, g1.got[-far], g1.got[far])
    cross_y = send(after(cotangent[0], *sent), back)
    wa = g1.whole()
    wide = 4 * heads * HEAD
    gb = wa[:, :, wide : wide + 4].reshape(width, 4).astype(F32).T

    a1, qkv = project(core_arg, after(x_own, *sent), x_oth, gb, wa)
    sent = g2.step(2, qkv)
    mixed0, logs0 = attend(slopes, after(qkv, *sent, cross_y), seg_col, 0, 2)
    sent = g2.step(3, mixed0)
    w2 = lax.all_gather(after(low_back, *sent), both)
    w2 = w2.reshape(2 * chips, 2, *w2.shape[1:])
    mixed1, logs1 = attend(slopes, after(qkv, *sent), seg_col, 2, 2)
    y_own = jnp.where(at_home, cotangent[0], after(cross_y, mixed1))
    y_oth = send(y_own, to_core)
    sent = g2.step(4, mixed1)
    mixed = (after(mixed0, *sent, y_own), mixed1)
    part_recv = send(branch(core_arg, mixed, wa), to_core)
    part_own = branch(core_arg, (after(mixed[0], g2.got[far], g2.got[-far]), mixed[1]), wa, x_own)
    w1 = g2.whole()
    h1, a2_own = residual(after(part_own, w1), part_recv, gb)
    a2_oth = send(a2_own, to_core)
    hidden, slope, gw2 = up(core_arg, a2_own, a2_oth, y_own, y_oth, w1)
    r2 = reduce_chips(gw2)
    f_own, f_oth, d_own, d_oth, gw1 = down(core_arg, a2_own, a2_oth, after(y_own, gw2), y_oth, hidden, slope, w1, w2)
    r1 = reduce_chips(gw1)
    d_recv = send(d_oth, to_core)
    dh1, da_own, sums2 = through_norm(h1, d_own, d_recv, y_own, gb[1:2], True)
    da_oth = send(da_own, to_core)
    f_recv = send(after(f_oth, da_own), to_core)
    do, gwo = head_grad(core_arg, da_own, da_oth, mixed, wa)
    result = (h1 + f_own.astype(F32) + after(f_recv, do).astype(F32)).astype(BF)
    both_mixed = jnp.concatenate(mixed, axis=1)
    both_logs = jnp.concatenate([logs0, logs1], axis=0)
    grads = attend_back(slopes, after(qkv, do, result), do, both_mixed, both_logs, seg)
    d1_oth, d1_own = project_back(core_arg, after(tuple(grads), r2), wa)
    d1_recv = send(d1_oth, to_core)
    grad_back = to_owner(after(r2, d1_own).astype(F32))
    gwq = project_weight(after(a1, d1_own), gwo, grads)
    cross_result = send(after(result, grad_back), back)
    result = jnp.where(at_home, result, after(cross_result, gwq))
    rc = Reduce(gwq.reshape(chips, width // chips, -1))
    sent = rc.step(1)
    grad_tokens, sums1 = through_norm(x_own, after(d1_own, *sent, grad_back), d1_recv, dh1, gb[0:1], False)
    cross_tokens = send(grad_tokens, back)
    sent = rc.step(2, sums1)
    sent = rc.step(3, result)
    sent = rc.step(4, cross_tokens)
    grad_in = to_owner(after(r1, *sent).astype(F32))
    sums = after(jnp.concatenate([sums1[0:1], sums2[0:1], sums1[1:2], sums2[1:2]], axis=0), *sent)
    for pairs in (to_core, to_y, *hops):
        sums = sums + send(sums, pairs)
    r3 = to_owner(rc.total())
    grad_tokens = jnp.where(at_home, grad_tokens, cross_tokens)
    per = r3.shape[0]
    wide = 3 * heads * HEAD
    grad_qkv = r3[:, :wide].reshape(per, 3, -1).transpose(1, 0, 2)
    grad_out = r3[:, wide:].T
    sums = lax.dynamic_slice_in_dim(sums, dp_rank.astype(jnp.uint32) * norm_gains.shape[1], norm_gains.shape[1], 1)
    return (result[None], grad_tokens[None], grad_qkv, grad_out, grad_in, grad_back.T, sums[0:2], sums[2:4])


def solution(mesh):
    n_dp, n_tensor = mesh.shape["dp"], mesh.shape["tensor"]
    if n_dp == 16 and n_tensor == 2:
        grid = Mesh(mesh.devices.reshape(n_dp // 2, 2, n_tensor), ("chip", "core", "tensor"))
        body, dp = fast_shards, ("chip", "core")
    else:
        grid, body, dp = mesh, shards, "dp"
    return jax.shard_map(
        body,
        mesh=grid,
        in_specs=(
            P(dp, "tensor", None),
            P(dp, None),
            P(None, dp, "tensor"),
            P("tensor", dp),
            P(dp, "tensor"),
            P("tensor", dp),
            P(None, dp),
            P(None, dp),
            P(dp, "tensor", None),
        ),
        out_specs=(
            P(dp, "tensor", None),
            P(dp, "tensor", None),
            P(None, dp, "tensor"),
            P("tensor", dp),
            P(dp, "tensor"),
            P("tensor", dp),
            P(None, dp),
            P(None, dp),
        ),
        check_vma=False,
    )
```
